128 devices in a mesh: wide: 8 (over y, core), col: 16 (over z, x).
Axes of the slice: x: 4, y: 4, z: 4, core: 2. Of those that a mesh axis runs over, the one named last changes fastest.
Arguments:
- rhs: float32 [98304, 256], P(('wide', 'col')), may hold values from -6 to 6
- basis: bfloat16 [98304, 256], P(('wide', 'col')), may hold values from -0.21875 to 0.21875
- self_block: bfloat16 [98304, 768], P(('wide', 'col'))
- near_block: bfloat16 [128, 8, 768, 768], P(('wide', 'col')), may hold values from -0.0546875 to 0.0546875
- near_ids: int32 [128, 8], P(('wide', 'col')), may hold values from -1 to 127, as said below
- couplings: bfloat16 [128, 40, 256, 256], P(('wide', 'col')), may hold values from -0.09375 to 0.09375
- far_ids: int32 [128, 40], P(('wide', 'col')), may hold values from -1 to 127, as said below
- intersection_start: int32 [128, 2], P(('wide', 'col')), may hold values from 0 to 512
- schwarz_inverse: bfloat16 [128, 1280, 1280], P(('wide', 'col'))
Outputs:
- solution: float32 [98304, 256], P(('wide', 'col'))
The draws below stay inside these ranges and needn't reach their ends.
Inputs may be any that keep to these rules, and one draw needn't show every extreme that they name: `near_ids`: row c lists every cluster adjacent to cluster c on the grid (larger index distance 1; id = first index * 16 + second), ids first and -1 after them; rows of corner and edge clusters end in -1. `far_ids`: row c lists distinct clusters whose larger grid index distance from cluster c is 2 to 3, ids first and -1 after them; counts are ragged, and some rows list every such cluster. `intersection_start`: column 0 starts the rows taken by the domain of the cluster before along the second grid index, column 1 those taken by the one after.
All inputs are finite; a program needn't handle non-finite values.
Results may differ from the reference program's by a relative error of at most 0.0025.
The reference program's roundings to bfloat16 on the way count: a program that leaves them out, or rounds other values in their place, can miss the bound.
Values may be sent and summed in bfloat16 or wider, within the bound.
A program may use at most 128 MiB of HBM per device.

```python
import math
import jax
import jax.numpy as jnp
import numpy as np
from jax import lax

M = 768
K = 256
R = 256
OV = 256
REACH = 3
NEAR = 8
ITERS = 2
LMAX = 40
ORDER = 1280
WIDE_CLUSTERS = 8
COL_CLUSTERS = 16
CLUSTERS = 128
ROWS = 98304


def draw_self_block(key, part):
    row_pos = jnp.arange(ROWS)[:, None] % M
    col_pos = jnp.arange(M)[None, :]
    identity = (row_pos == col_pos).astype(jnp.float32)
    noise = 0.5 * jax.random.normal(key, (ROWS, M), jnp.float32) / math.sqrt(M)
    diag_scale = 2.0
    return (noise + diag_scale * identity).astype(jnp.bfloat16)


def draw_schwarz_inverse(key, part):
    identity = jnp.eye(ORDER, dtype=jnp.float32)[None]
    noise = 0.3 * jax.random.normal(key, (CLUSTERS, ORDER, ORDER), jnp.float32) / math.sqrt(ORDER)
    return (noise + identity).astype(jnp.bfloat16)


def grid_candidates(offsets):
    cluster_ids = jnp.arange(CLUSTERS)
    wide_pos = cluster_ids // COL_CLUSTERS
    col_pos = cluster_ids % COL_CLUSTERS
    steps_arr = jnp.asarray(offsets, jnp.int32)
    new_wide = wide_pos[:, None] + steps_arr[None, :, 0]
    new_col = col_pos[:, None] + steps_arr[None, :, 1]
    inside = (new_wide >= 0) & (new_wide < WIDE_CLUSTERS) & (new_col >= 0) & (new_col < COL_CLUSTERS)
    return (new_wide * COL_CLUSTERS + new_col, inside)


def draw_near_ids(key, part):
    offsets = np.array([(a, b) for a in range(-1, 2) for b in range(-1, 2) if not (a == 0 and b == 0)], np.int32)
    count_all = offsets.shape[0]
    candidates, inside = grid_candidates(offsets)
    scores = jax.random.randint(key, (CLUSTERS, count_all), 0, 1 << 20) * 8 + jnp.arange(count_all)
    scores = jnp.where(inside, scores, -1 - jnp.arange(count_all))
    top_scores, order = lax.top_k(scores, NEAR)
    picked = jnp.take_along_axis(candidates, order, axis=1)
    return jnp.where(top_scores >= 0, picked, -1).astype(jnp.int32)


def draw_far_ids(key, part):
    offsets = np.array([(a, b) for a in range(-REACH, REACH + 1) for b in range(-REACH, REACH + 1) if max(abs(a), abs(b)) >= 2], np.int32)
    candidates, inside = grid_candidates(offsets)
    key_scores = jax.random.fold_in(key, 11)
    key_count = jax.random.fold_in(key, 12)
    key_hot = jax.random.fold_in(key, 13)
    scores = jax.random.randint(key_scores, (CLUSTERS, LMAX), 0, 1 << 20) * 64 + jnp.arange(LMAX)
    scores = jnp.where(inside, scores, -1 - jnp.arange(LMAX))
    top_scores, order = lax.top_k(scores, LMAX)
    picked = jnp.take_along_axis(candidates, order, axis=1)
    live_total = jnp.sum(inside.astype(jnp.int32), axis=1)
    drawn_count = jax.random.randint(key_count, (CLUSTERS,), 4, 24)
    is_hot = jax.random.randint(key_hot, (CLUSTERS,), 0, 8) == 0
    cluster_ids = jnp.arange(CLUSTERS)
    middle = cluster_ids == WIDE_CLUSTERS // 2 * COL_CLUSTERS + COL_CLUSTERS // 2
    counts = jnp.where(is_hot | middle, live_total, jnp.minimum(drawn_count, live_total))
    ranks = jnp.arange(LMAX)[None, :]
    return jnp.where(ranks < counts[:, None], picked, -1).astype(jnp.int32)


def plant(values, own_key, smallest, top_value):
    longest = values.shape.index(max(values.shape))
    spots = []
    for shift in (0, 1):
        where = [jax.random.randint(jax.random.fold_in(own_key, axis), (), 0, length) for axis, length in enumerate(values.shape)]
        where[longest] = (where[longest] + shift) % values.shape[longest]
        spots.append(tuple(where))
    return values.at[spots[0]].set(smallest).at[spots[1]].set(top_value)


def block_scale(key, shape, shards, smallest, largest):
    level, own = 1.0, jax.random.fold_in(key, 6)
    for dim, parts in shards:
        draws = jnp.exp(jax.random.uniform(jax.random.fold_in(own, dim), (parts,), jnp.float32, smallest / len(shards), largest / len(shards)))
        level = level * jnp.repeat(draws, shape[dim] // parts).reshape([-1 if axis == dim else 1 for axis in range(len(shape))])
    return level


def bell_draw(key, extent, deviation, most, pieces=(), held_as=jnp.bfloat16):
    gain = block_scale(key, extent, pieces, -0.22, 0.18) if pieces else 1.0
    values = jax.random.normal(key, extent, jnp.float32) * deviation * gain
    return jnp.minimum(jnp.maximum(values, -most), most).astype(held_as)


def setup_inputs(seed: int = 0) -> dict:
    streams_of = jax.random.split(jax.random.key(seed), 10)
    rhs = bell_draw(streams_of[0], (ROWS, K), 1.0, 6.0, ((0, 128),), jnp.float32)
    basis = bell_draw(streams_of[1], (ROWS, R), M ** -0.5, 0.21875, ((0, 128),))
    self_block = draw_self_block(jax.random.fold_in(streams_of[9], 71), 0)
    near_block = bell_draw(streams_of[3], (CLUSTERS, NEAR, M, M), (16 * M) ** -0.5, 0.0546875, ((0, 128),))
    near_ids = draw_near_ids(jax.random.fold_in(streams_of[9], 71), 0)
    couplings = bell_draw(streams_of[5], (CLUSTERS, LMAX, R, R), (16 * R) ** -0.5, 0.09375, ((0, 128),))
    far_ids = draw_far_ids(jax.random.fold_in(streams_of[9], 71), 0)
    intersection_start = plant(jax.random.randint(streams_of[7], (CLUSTERS, 2), 0, M - OV + 1), jax.random.fold_in(streams_of[7], 1), 0, M - OV).astype(jnp.int32)
    schwarz_inverse = draw_schwarz_inverse(jax.random.fold_in(streams_of[9], 71), 0)
    return {"rhs": rhs, "basis": basis, "self_block": self_block, "near_block": near_block, "near_ids": near_ids, "couplings": couplings, "far_ids": far_ids, "intersection_start": intersection_start, "schwarz_inverse": schwarz_inverse}


HIGHEST_PREC = lax.Precision.HIGHEST

def gram_of(left, right):
    return jnp.einsum('nk,nj->kj', left, right, precision=HIGHEST_PREC)

def lower_solve(factor, matrix):
    return lax.linalg.triangular_solve(factor, matrix, left_side=False, lower=True, transpose_a=True)

def apply_operator(vector_in, basis, self_block, near_block, near_ids, couplings, far_ids):
    rounded = vector_in.astype(jnp.bfloat16).reshape(CLUSTERS, M, K)
    basis_c = basis.reshape(CLUSTERS, M, R)
    self_c = self_block.reshape(CLUSTERS, M, M)
    coefficients = jnp.einsum('cmr,cmk->crk', basis_c.astype(jnp.float32), rounded.astype(jnp.float32)).astype(jnp.bfloat16)

    def one_cluster(inputs):
        self_m, near_m, near_row, coupling_row, far_row, basis_m, own_vec = inputs
        result = jnp.dot(self_m.astype(jnp.float32), own_vec.astype(jnp.float32), preferred_element_type=jnp.float32)
        for slot_index in range(NEAR):
            neighbour = near_row[slot_index]
            other = rounded[jnp.maximum(neighbour, 0)]
            product = jnp.dot(near_m[slot_index].astype(jnp.float32), other.astype(jnp.float32), preferred_element_type=jnp.float32)
            result = result + jnp.where(neighbour >= 0, product, jnp.zeros_like(product))
        picked = coefficients[jnp.maximum(far_row, 0)]
        weighted = jnp.where((far_row >= 0)[:, None, None], coupling_row, jnp.zeros_like(coupling_row))
        far_sum = jnp.einsum('lrs,lsk->rk', weighted.astype(jnp.float32), picked.astype(jnp.float32))
        result = result + jnp.dot(basis_m.astype(jnp.float32), far_sum.astype(jnp.bfloat16).astype(jnp.float32), preferred_element_type=jnp.float32)
        return result
    outcome = lax.map(one_cluster, (self_c, near_block, near_ids, couplings, far_ids, basis_c, rounded))
    return outcome.reshape(ROWS, K)

def precondition(vector_in, intersection_start, schwarz_inverse):
    rounded = vector_in.astype(jnp.bfloat16).reshape(CLUSTERS, M, K)
    position = jnp.arange(CLUSTERS) % COL_CLUSTERS
    has_prev = (position > 0)[:, None, None]
    has_next = (position < COL_CLUSTERS - 1)[:, None, None]

    def window(matrix, start):
        return lax.dynamic_slice_in_dim(matrix, start, OV, 0)
    bottoms = jax.vmap(window)(rounded, intersection_start[:, 1])
    tops = jax.vmap(window)(rounded, intersection_start[:, 0])
    prev_rows = jnp.where(has_prev, jnp.roll(bottoms, 1, axis=0), jnp.zeros_like(bottoms))
    next_rows = jnp.where(has_next, jnp.roll(tops, -1, axis=0), jnp.zeros_like(tops))
    domain = jnp.concatenate([prev_rows, rounded, next_rows], axis=1)
    solved = lax.map(lambda pair: jnp.dot(pair[0].astype(jnp.float32), pair[1].astype(jnp.float32), preferred_element_type=jnp.float32), (schwarz_inverse, domain))
    result = solved[:, OV:OV + M]
    to_prev = solved[:, :OV]
    to_next = solved[:, OV + M:]
    from_next = jnp.where(has_next, jnp.roll(to_prev, -1, axis=0), jnp.zeros_like(to_prev))
    from_prev = jnp.where(has_prev, jnp.roll(to_next, 1, axis=0), jnp.zeros_like(to_next))

    def place(matrix, addend, start):
        current = lax.dynamic_slice_in_dim(matrix, start, OV, 0)
        return lax.dynamic_update_slice_in_dim(matrix, current + addend, start, 0)
    result = jax.vmap(place)(result, from_next, intersection_start[:, 1])
    result = jax.vmap(place)(result, from_prev, intersection_start[:, 0])
    return result.reshape(ROWS, K)

def reference(rhs, basis, self_block, near_block, near_ids, couplings, far_ids, intersection_start, schwarz_inverse):
    factor = jnp.linalg.cholesky(gram_of(rhs, rhs))
    beta_block = factor.T
    bases = [lower_solve(factor, rhs)]
    directions = []
    columns = []
    for iteration in range(ITERS):
        precond_out = precondition(bases[-1], intersection_start, schwarz_inverse)
        image = apply_operator(precond_out, basis, self_block, near_block, near_ids, couplings, far_ids)
        stacked = jnp.concatenate(bases, axis=1)
        projected = gram_of(stacked, image)
        image = image - jnp.dot(stacked, projected, precision=HIGHEST_PREC)
        factor = jnp.linalg.cholesky(gram_of(image, image))
        columns.append((projected, factor.T))
        directions.append(precond_out)
        if iteration + 1 < ITERS:
            bases.append(lower_solve(factor, image))
    hessen = jnp.zeros(((ITERS + 1) * K, ITERS * K), jnp.float32)
    for column_index, (projected, sub_block) in enumerate(columns):
        upper_rows = (column_index + 1) * K
        hessen = hessen.at[:upper_rows, column_index * K:(column_index + 1) * K].set(projected)
        hessen = hessen.at[upper_rows:upper_rows + K, column_index * K:(column_index + 1) * K].set(sub_block)
    normal_matrix = jnp.dot(hessen.T, hessen, precision=HIGHEST_PREC)
    target = jnp.dot(hessen[:K].T, beta_block, precision=HIGHEST_PREC)
    small_factor = jnp.linalg.cholesky(normal_matrix)
    middle = lax.linalg.triangular_solve(small_factor, target, left_side=True, lower=True)
    weights_y = lax.linalg.triangular_solve(small_factor, middle, left_side=True, lower=True, transpose_a=True)
    return jnp.dot(jnp.concatenate(directions, axis=1), weights_y, precision=HIGHEST_PREC)
```

```python
import functools

import jax
import jax.numpy as jnp
from jax import lax
from jax.experimental import pallas as pl
from jax.experimental.pallas import tpu as pltpu
from jax.sharding import PartitionSpec as P

REACH = 3
SPAN = 2 * REACH + 1
MESH = pl.DeviceIdType.MESH
HIGHEST = lax.Precision.HIGHEST
F32 = jnp.float32
BF16 = jnp.bfloat16
VMEM_BYTES = 60 * 1024 * 1024


def dot(left, right):
    return jnp.dot(left, right, preferred_element_type=F32)


def dot_full(left, right):
    return jnp.dot(left, right, precision=HIGHEST, preferred_element_type=F32)


def dot_full_t(left, right):
    return lax.dot_general(
        left, right, (((1,), (1,)), ((), ())), precision=HIGHEST, preferred_element_type=F32
    )


def t_dot_full(left, right):
    return lax.dot_general(
        left, right, (((0,), (0,)), ((), ())), precision=HIGHEST, preferred_element_type=F32
    )


def picks(start, count, total):
    row = lax.broadcasted_iota(jnp.int32, (count, total), 0)
    lane = lax.broadcasted_iota(jnp.int32, (count, total), 1)
    return jnp.where(lane - row == start, 1.0, 0.0).astype(BF16)


def places(start, count, total):
    row = lax.broadcasted_iota(jnp.int32, (total, count), 0)
    lane = lax.broadcasted_iota(jnp.int32, (total, count), 1)
    return jnp.where(row - lane == start, 1.0, 0.0).astype(BF16)


def three_parts(value):
    high = value.astype(BF16)
    rest = value - high.astype(F32)
    mid = rest.astype(BF16)
    return high, mid, (rest - mid.astype(F32)).astype(BF16)


def remote(src, dst, send_sem, recv_sem, w, c):
    return pltpu.make_async_remote_copy(
        src_ref=src,
        dst_ref=dst,
        send_sem=send_sem,
        recv_sem=recv_sem,
        device_id=(w, c),
        device_id_type=MESH,
    )


def greet(w, c, wide, col):
    barrier = pltpu.get_barrier_semaphore()

    def along_col(k, carry):
        pl.semaphore_signal(
            barrier, inc=1, device_id=(w, lax.rem(c + k, col)), device_id_type=MESH
        )
        return carry

    def along_wide(k, carry):
        pl.semaphore_signal(
            barrier, inc=1, device_id=(lax.rem(w + k, wide), c), device_id_type=MESH
        )
        return carry

    lax.fori_loop(1, col, along_col, 0)
    lax.fori_loop(1, wide, along_wide, 0)


def meet(wide, col):
    pl.semaphore_wait(pltpu.get_barrier_semaphore(), wide + col - 2)


def all_reduce(w, c, wide, col, g, half, land, ysl, out, send, recv):
    rows = g.shape[0]
    high = rows // 2
    part = high // col
    core = lax.rem(w, 2)
    y = w // 2
    ys = wide // 2
    partner = w + 1 - 2 * core
    mine = pl.multiple_of(core * high, high)
    other = pl.multiple_of((1 - core) * high, high)
    own = pl.multiple_of(mine + c * part, part)

    swap = remote(g.at[pl.ds(other, high)], half, send.at[0], recv.at[0], partner, c)
    swap.start()
    swap.wait()
    g[pl.ds(mine, high), :] += half[...]

    def scatter(k, carry):
        d = lax.rem(c + k, col)
        remote(
            g.at[pl.ds(pl.multiple_of(mine + d * part, part), part)],
            land.at[pl.ds(pl.multiple_of((col - 1 - k) * part, part), part)],
            send.at[1],
            recv.at[1],
            w,
            d,
        ).start()
        return carry

    lax.fori_loop(1, col, scatter, 0)
    many = (col - 1) * part
    remote(g.at[pl.ds(0, many)], land, send.at[1], recv.at[1], w, c).wait()
    total = g[pl.ds(own, part), :]
    for k in range(col - 1):
        total += land[k * part : (k + 1) * part, :]
    ysl[y] = total

    def spread(k, carry):
        other_y = lax.rem(y + k, ys)
        remote(ysl.at[y], ysl.at[y], send.at[2], recv.at[2], 2 * other_y + core, c).start()
        return carry

    lax.fori_loop(1, ys, spread, 0)
    few = pl.ds(0, ys - 1)
    remote(ysl.at[few], ysl.at[few], send.at[2], recv.at[2], w, c).wait()
    total = ysl[0]
    for k in range(1, ys):
        total += ysl[k]
    out[pl.ds(own, part), :] = total

    def gather(k, carry):
        d = lax.rem(c + k, col)
        spot = pl.ds(own, part)
        remote(out.at[spot], out.at[spot], send.at[3], recv.at[3], w, d).start()
        return carry

    lax.fori_loop(1, col, gather, 0)
    spot = pl.ds(0, many)
    remote(out.at[spot], out.at[spot], send.at[3], recv.at[3], w, c).wait()
    spot = pl.ds(mine, high)
    swap = remote(out.at[spot], out.at[spot], send.at[4], recv.at[4], partner, c)
    swap.start()
    swap.wait()


def reduce_scratch(rows, width, wide, col):
    high = rows // 2
    part = high // col
    return [
        pltpu.VMEM((rows, width), F32),
        pltpu.VMEM((high, width), F32),
        pltpu.VMEM(((col - 1) * part, width), F32),
        pltpu.VMEM((wide // 2, part, width), F32),
        pltpu.SemaphoreType.DMA((5,)),
        pltpu.SemaphoreType.DMA((5,)),
    ]


def local_grams(lefts, right, g, step):
    width = right.shape[1]
    rows = right.shape[0]
    for i, left in enumerate(lefts):
        spot = slice(i * width, (i + 1) * width)
        g[spot, :] = t_dot_full(left[0:step, :], right[0:step, :])

        def add(k, carry, left=left, spot=spot):
            piece = pl.ds(pl.multiple_of(k * step, step), step)
            g[spot, :] += t_dot_full(left[piece, :], right[piece, :])
            return carry

        lax.fori_loop(1, rows // step, add, 0)


def first_gram_kernel(wide, col, step, rhs, out, g, half, land, ysl, send, recv):
    w, c = lax.axis_index("wide"), lax.axis_index("col")
    greet(w, c, wide, col)
    local_grams([rhs], rhs, g, step)
    meet(wide, col)
    all_reduce(w, c, wide, col, g, half, land, ysl, out, send, recv)


def step_kernel(wide, col, step, first, *refs):
    if first:
        (starts, near_ids, far_ids, x, mt, basis_h, self_h, near_h, coup_h, sch_h, *rest) = refs
        (v, z, wv, gram, *rest) = rest
    else:
        (starts, near_ids, far_ids, x, mt, vprev, u, basis_h, self_h, near_h, coup_h, sch_h, *rest) = refs
        (z, gram, v, wv, *rest) = rest
    (basis, selfb, near, coup, sch, stage, dom, pad_next, pad_prev, edge, nb, win, far, *rest) = rest
    (load, hs, hr, ns, nr, ws, wr, rs, rr, ps, pr, *reduce) = rest
    g, half, land, ysl, send, recv = reduce
    w, c = lax.axis_index("wide"), lax.axis_index("col")
    core = lax.rem(w, 2)
    partner = w + 1 - 2 * core
    rows, width = x.shape
    margin = edge.shape[1]
    has_prev, has_next = c > 0, c < col - 1

    loads = [
        pltpu.make_async_copy(sch_h.at[0], sch, load.at[0]),
        pltpu.make_async_copy(basis_h, basis, load.at[1]),
        pltpu.make_async_copy(self_h, selfb, load.at[2]),
        pltpu.make_async_copy(near_h.at[0], near, load.at[3]),
        pltpu.make_async_copy(coup_h.at[0], coup, load.at[4]),
    ]
    for copy in loads:
        copy.start()

    @pl.when(jnp.logical_not(has_prev))
    def _():
        dom[0:margin, :] = jnp.zeros((margin, width), BF16)
        pad_prev[...] = jnp.zeros((margin, width), F32)

    @pl.when(jnp.logical_not(has_next))
    def _():
        dom[margin + rows :, :] = jnp.zeros((margin, width), BF16)
        pad_next[...] = jnp.zeros((margin, width), F32)

    greet(w, c, wide, col)

    def make_v(k, carry):
        piece = pl.ds(pl.multiple_of(k * step, step), step)
        value = dot_full(x[piece, :], mt[...])
        if not first:
            value += dot_full(vprev[piece, :], u[...])
        v[piece, :] = value
        dom[pl.ds(pl.multiple_of(margin + k * step, step), step), :] = value.astype(BF16)
        return carry

    lax.fori_loop(0, rows // step, make_v, 0)
    start_prev, start_next = starts[0, 0], starts[0, 1]
    stage[0] = dot(picks(start_next, margin, rows), dom[margin : margin + rows, :]).astype(BF16)
    stage[1] = dot(picks(start_prev, margin, rows), dom[margin : margin + rows, :]).astype(BF16)
    meet(wide, col)

    to_next = remote(stage.at[0], dom.at[pl.ds(0, margin)], hs.at[0], hr.at[0], w, c + 1)
    to_prev = remote(
        stage.at[1], dom.at[pl.ds(margin + rows, margin)], hs.at[1], hr.at[1], w, c - 1
    )
    out_prev = remote(
        edge.at[0], pad_next, hs.at[2], hr.at[2], w, c - 1
    )
    out_next = remote(
        edge.at[1], pad_prev, hs.at[3], hr.at[3], w, c + 1
    )
    pl.when(has_next)(to_next.start)
    pl.when(has_prev)(to_prev.start)

    nb[9] = jnp.zeros((rows, width), BF16)
    win[SPAN * SPAN] = jnp.zeros(win.shape[1:], BF16)

    loads[0].wait()
    pl.when(has_prev)(to_next.wait_recv)
    pl.when(has_next)(to_prev.wait_recv)
    edge[0] = dot(sch[0:margin, :], dom[...])
    pl.when(has_prev)(out_prev.start)
    edge[1] = dot(sch[margin + rows :, :], dom[...])
    pl.when(has_next)(out_next.start)

    def solve(k, carry):
        piece = pl.ds(pl.multiple_of(k * step, step), step)
        z[piece, :] = dot(sch[pl.ds(pl.multiple_of(margin + k * step, step), step), :], dom[...])
        return carry

    lax.fori_loop(0, rows // step, solve, 0)
    pl.when(has_next)(out_prev.wait_recv)
    pl.when(has_prev)(out_next.wait_recv)
    for start, pad in ((start_next, pad_next), (start_prev, pad_prev)):
        spread = places(start, margin, rows)
        for part in three_parts(pad[...]):
            z[...] += dot(spread, part)
    nb[4] = z[...].astype(BF16)
    loads[1].wait()

    def near_to(dw, dc, source):
        return remote(
            nb.at[source], nb.at[(1 - dw) * 3 + dc + 1], ns.at[(1 - dw) * 3 + dc + 1],
            nr.at[(1 - dw) * 3 + dc + 1], w + dw, c,
        )

    def near_col(dc):
        return remote(nb.at[4], nb.at[4 - dc], ns.at[4 - dc], nr.at[4 - dc], w, c + dc)

    beside = {-1: has_prev, 1: has_next}
    within = {d: (w + d >= 0) & (w + d < wide) for d in range(-REACH, REACH + 1) if d}
    for d in (-1, 1):
        pl.when(beside[d])(near_col(d).start)
    for d in (-1, 1):
        pl.when(within[d])(near_to(d, 0, 4).start)

    centre = REACH * SPAN + REACH
    win[centre] = lax.dot_general(
        basis[...], nb[4], (((0,), (0,)), ((), ())), preferred_element_type=F32
    ).astype(BF16)

    def far_wide(d):
        return remote(
            win.at[centre], win.at[centre - d], ws.at[REACH - d], wr.at[REACH - d], w + d, c
        )

    for d in (1, -1, 2, -2, 3, -3):
        pl.when(within[d])(far_wide(d).start)

    loads[2].wait()

    def own_part(k, carry):
        piece = pl.ds(pl.multiple_of(k * step, step), step)
        wv[piece, :] = dot(selfb[piece, :], nb[4])
        return carry

    lax.fori_loop(0, rows // step, own_part, 0)

    for d in within:
        pl.when(within[-d])(far_wide(d).wait_recv)

    def strip_to(direction, k):
        held = REACH - direction * (k - 1)
        lands = held - direction
        rows_of = lambda i: pl.ds(i * SPAN + REACH * core, REACH + 1)
        sem = lands
        return remote(
            win.at[rows_of(held)], win.at[rows_of(lands)], rs.at[sem], rr.at[sem], w, c + direction
        )

    def share(i):
        return remote(
            win.at[pl.ds(i * SPAN + 1 + 2 * core, REACH)],
            win.at[pl.ds(i * SPAN + (REACH + 1) * core, REACH)],
            ps.at[i], pr.at[i], partner, c,
        )

    def arrives(direction, k):
        return c - k >= 0 if direction > 0 else c + k < col

    def sends(direction, k):
        held = c - (k - 1) >= 0 if direction > 0 else c + (k - 1) < col
        return held & beside[direction]

    for d in (1, -1):
        pl.when(sends(d, 1))(strip_to(d, 1).start)

    for d in (-1, 1):
        pl.when(beside[d])(near_col(-d).wait_recv)
        for e in (-1, 1):
            pl.when(beside[d] & within[e])(near_to(e, d, 4 + d).start)

    for k in range(1, REACH + 1):
        for d in (1, -1):
            pl.when(arrives(d, k))(strip_to(d, k).wait_recv)
            if k < REACH:
                pl.when(sends(d, k + 1))(strip_to(d, k + 1).start)
            pl.when(arrives(d, k))(share(REACH - d * k).start)
        if k == 1:
            for e in (-1, 1):
                for d in (-1, 0, 1):
                    ok = within[-e] if d == 0 else within[-e] & beside[d]
                    pl.when(ok)(near_to(e, d, 4 + d).wait_recv)
            loads[3].wait()

            def near_slot(s, carry):
                cluster = near_ids[0, s]
                place = (lax.div(cluster, col) - w + 1) * 3 + (lax.rem(cluster, col) - c + 1)
                place = jnp.where(cluster >= 0, jnp.minimum(jnp.maximum(place, 0), 8), 9)

                def near_rows(r, inner):
                    piece = pl.ds(pl.multiple_of(r * step, step), step)
                    wv[piece, :] += dot(near[s, piece, :], nb[place])
                    return inner

                return lax.fori_loop(0, rows // step, near_rows, carry)

            lax.fori_loop(0, near_ids.shape[1], near_slot, 0)
    for k in range(1, REACH + 1):
        for d in (1, -1):
            pl.when(arrives(d, k))(share(REACH - d * k).wait_recv)
    loads[4].wait()
    far[...] = jnp.zeros_like(far)

    def far_slot(s, carry):
        cluster = far_ids[0, s]
        place = (lax.rem(cluster, col) - c + REACH) * SPAN + (lax.div(cluster, col) - w + REACH)
        place = jnp.where(cluster >= 0, jnp.minimum(jnp.maximum(place, 0), SPAN * SPAN - 1), SPAN * SPAN)
        far[...] += dot(coup[s], win[place])
        return carry

    lax.fori_loop(0, far_ids.shape[1], far_slot, 0)
    far_b = far[...].astype(BF16)

    def basis_part(k, carry):
        piece = pl.ds(pl.multiple_of(k * step, step), step)
        wv[piece, :] += dot(basis[piece, :], far_b)
        return carry

    lax.fori_loop(0, rows // step, basis_part, 0)
    local_grams([v, wv] if first else [vprev, x, wv], wv, g, step)

    pl.when(has_next)(to_next.wait_send)
    pl.when(has_prev)(to_prev.wait_send)
    pl.when(has_prev)(out_prev.wait_send)
    pl.when(has_next)(out_next.wait_send)
    for d in (-1, 1):
        pl.when(beside[d])(near_col(d).wait_send)
        pl.when(within[d])(near_to(d, 0, 4).wait_send)
        for e in (-1, 1):
            pl.when(beside[d] & within[e])(near_to(e, d, 4 + d).wait_send)
    for d in within:
        pl.when(within[d])(far_wide(d).wait_send)
    for k in range(1, REACH + 1):
        for d in (1, -1):
            pl.when(sends(d, k))(strip_to(d, k).wait_send)
            pl.when(arrives(d, k))(share(REACH - d * k).wait_send)

    all_reduce(w, c, wide, col, g, half, land, ysl, gram, send, recv)


def inverse_factors(matrices, scratch):
    n = matrices[0].shape[0]
    row = lax.broadcasted_iota(jnp.int32, (n, n), 0)
    lane = lax.broadcasted_iota(jnp.int32, (n, n), 1)
    eye = (row == lane).astype(F32)

    def lower(e):
        return jnp.where(row > lane, e, 0.5 * e * eye)

    scaled, scales = [], []
    for i, a in enumerate(matrices):
        only = a * eye
        by_row = lax.rsqrt(jnp.sum(only, axis=1, keepdims=True))
        by_lane = lax.rsqrt(jnp.sum(only, axis=0, keepdims=True))
        a = a * by_row * by_lane
        scratch[i] = eye - lower(a - eye)
        scaled.append(a)
        scales.append(by_lane)
    limit = 1e-5

    def go_on(state):
        step, error = state
        return (step < 8) & jnp.logical_not(error < limit)

    def refine(state):
        step, _ = state
        error = jnp.float32(0.0)
        for i, a in enumerate(scaled):
            m = scratch[i]
            e = dot_full_t(dot_full(m, a), m) - eye
            scratch[i] = m - dot_full(lower(e), m)
            error = error + jnp.sum(e * e)
        return step + 1, error

    _, error = lax.while_loop(go_on, refine, (jnp.int32(0), jnp.float32(1.0)))

    @pl.when(jnp.logical_not(error < limit))
    def _():
        for i, a in enumerate(scaled):

            def eliminate(j, state):
                s, m = state
                at_lane = jnp.sum(jnp.where(lane == j, s, 0.0), axis=1, keepdims=True)
                at_row = jnp.sum(jnp.where(row == j, s, 0.0), axis=0, keepdims=True)
                m_row = jnp.sum(jnp.where(row == j, m, 0.0), axis=0, keepdims=True)
                pivot = jnp.sum(jnp.where(row == j, at_lane, 0.0), axis=0, keepdims=True)
                pivot = pivot[:, 0:1]
                times = jnp.where(row[:, 0:1] > j, at_lane / pivot, 0.0)
                s = s - times * at_row
                m = m - times * m_row
                m = jnp.where(row == j, m_row * lax.rsqrt(pivot), m)
                return s, m

            _, m = lax.fori_loop(0, n, eliminate, (a, eye))
            scratch[i] = m

    for i, by_lane in enumerate(scales):
        scratch[i] = scratch[i] * by_lane


def first_factor_kernel(g0, m, mt):
    inverse_factors([g0[...]], m)
    mt[...] = m[0].T


def second_factor_kernel(gram, m, mt, u):
    k = gram.shape[1]
    h = gram[0:k, :]
    n = gram[k:, :]
    inverse_factors([n - t_dot_full(h, h), n], m)
    mt[...] = m[0].T
    u[...] = -dot_full(h, mt[...])


def last_kernel(step, g0, m0, gram1, mn, gram2, z1, z2, out, m):
    k = g0.shape[1]
    beta = dot_full(m0[0], g0[...])
    h1, h2 = gram1[0:k, :], gram2[0:k, :]
    n12, n22 = gram2[k : 2 * k, :], gram2[2 * k :, :]
    first = mn[1]
    b1 = dot_full(first, t_dot_full(h1, beta))
    t = dot_full(first, n12)
    inverse_factors([n22 - t_dot_full(t, t)], m)
    b2 = t_dot_full(h2, beta) - t_dot_full(t, b1)
    y2 = t_dot_full(m[0], dot_full(m[0], b2))
    y1 = t_dot_full(first, b1 - dot_full(t, y2))

    def combine(i, carry):
        piece = pl.ds(pl.multiple_of(i * step, step), step)
        out[piece, :] = dot_full(z1[piece, :], y1) + dot_full(z2[piece, :], y2)
        return carry

    lax.fori_loop(0, out.shape[0] // step, combine, 0)


def on_device(
    wide, col, rhs, basis, self_block, near_block, near_ids, couplings, far_ids, starts, schwarz_inverse
):
    rows, width = rhs.shape
    rank = basis.shape[1]
    order = schwarz_inverse.shape[1]
    margin = (order - rows) // 2
    step = rows // 3
    slots, links = near_ids.shape[1], far_ids.shape[1]
    vmem = pl.BlockSpec(memory_space=pltpu.VMEM)
    smem = pl.BlockSpec(memory_space=pltpu.SMEM)
    anywhere = pl.BlockSpec(memory_space=pl.ANY)

    def block(n):
        return jax.ShapeDtypeStruct((n, width), F32)

    square = jax.ShapeDtypeStruct((1, width, width), F32)
    local = pltpu.CompilerParams(vmem_limit_bytes=VMEM_BYTES)

    def talks(number):
        return pltpu.CompilerParams(
            collective_id=number, has_side_effects=True, vmem_limit_bytes=VMEM_BYTES
        )

    gram0 = pl.pallas_call(
        functools.partial(first_gram_kernel, wide, col, step),
        out_shape=block(width),
        in_specs=[vmem],
        out_specs=vmem,
        scratch_shapes=reduce_scratch(width, width, wide, col),
        compiler_params=talks(0),
        name="first_gram",
    )(rhs)
    m0, mt0 = pl.pallas_call(
        first_factor_kernel,
        out_shape=(square, block(width)),
        in_specs=[vmem],
        out_specs=(vmem, vmem),
        compiler_params=local,
        name="first_factor",
    )(gram0)

    def take_step(first, *blocks):
        grams = 2 if first else 3
        outs = [block(rows)] * 3 if first else [block(rows)]
        held = [] if first else [pltpu.VMEM((rows, width), F32)] * 2
        dma = pltpu.SemaphoreType.DMA
        return pl.pallas_call(
            functools.partial(step_kernel, wide, col, step, first),
            out_shape=(*outs, block(grams * width)),
            in_specs=[smem] * 3 + [vmem] * len(blocks) + [anywhere] * 5,
            out_specs=(vmem,) * (len(outs) + 1),
            scratch_shapes=held
            + [
                pltpu.VMEM((rows, rank), BF16),
                pltpu.VMEM((rows, rows), BF16),
                pltpu.VMEM((slots, rows, rows), BF16),
                pltpu.VMEM((links, rank, rank), BF16),
                pltpu.VMEM((order, order), BF16),
                pltpu.VMEM((2, margin, width), BF16),
                pltpu.VMEM((order, width), BF16),
                pltpu.VMEM((margin, width), F32),
                pltpu.VMEM((margin, width), F32),
                pltpu.VMEM((2, margin, width), F32),
                pltpu.VMEM((10, rows, width), BF16),
                pltpu.VMEM((SPAN * SPAN + 1, rank, width), BF16),
                pltpu.VMEM((rank, width), F32),
                dma((5,)),
                dma((4,)),
                dma((4,)),
                dma((9,)),
                dma((9,)),
                dma((SPAN,)),
                dma((SPAN,)),
                dma((SPAN,)),
                dma((SPAN,)),
                dma((SPAN,)),
                dma((SPAN,)),
            ]
            + reduce_scratch(grams * width, width, wide, col),
            compiler_params=talks(1 if first else 2),
            name="first_step" if first else "second_step",
        )(starts, near_ids, far_ids, *blocks, basis, self_block, near_block, couplings, schwarz_inverse)

    v1, z1, w1, gram1 = take_step(True, rhs, mt0)
    m1, mt1, u = pl.pallas_call(
        second_factor_kernel,
        out_shape=(jax.ShapeDtypeStruct((2, width, width), F32), block(width), block(width)),
        in_specs=[vmem],
        out_specs=(vmem,) * 3,
        compiler_params=local,
        name="second_factor",
    )(gram1)
    z2, gram2 = take_step(False, w1, mt1, v1, u)
    return pl.pallas_call(
        functools.partial(last_kernel, step),
        out_shape=block(rows),
        in_specs=[vmem] * 7,
        out_specs=vmem,
        scratch_shapes=[pltpu.VMEM((1, width, width), F32)],
        compiler_params=local,
        name="last",
    )(gram0, m0, gram1, m1, gram2, z1, z2)


def solution(mesh):
    in_specs = (
        P(("wide", "col"), None),
        P(("wide", "col"), None),
        P(("wide", "col"), None),
        P(("wide", "col"), None, None, None),
        P(("wide", "col"), None),
        P(("wide", "col"), None, None, None),
        P(("wide", "col"), None),
        P(("wide", "col"), None),
        P(("wide", "col"), None, None),
    )
    out_specs = P(("wide", "col"), None)
    return jax.shard_map(
        functools.partial(on_device, mesh.shape["wide"], mesh.shape["col"]),
        mesh=mesh,
        in_specs=in_specs,
        out_specs=out_specs,
        check_vma=False,
    )
```

```python
import functools

import jax
import jax.numpy as jnp
from jax import lax
from jax.experimental import pallas as pl
from jax.experimental.pallas import tpu as pltpu
from jax.sharding import PartitionSpec as P

REACH = 3
SPAN = 2 * REACH + 1
MESH = pl.DeviceIdType.MESH
HIGHEST = lax.Precision.HIGHEST
F32 = jnp.float32
BF16 = jnp.bfloat16
VMEM_BYTES = 60 * 1024 * 1024


def dot(left, right):
    return jnp.dot(left, right, preferred_element_type=F32)


def dot_full(left, right):
    return jnp.dot(left, right, precision=HIGHEST, preferred_element_type=F32)


def dot_full_t(left, right):
    return lax.dot_general(
        left, right, (((1,), (1,)), ((), ())), precision=HIGHEST, preferred_element_type=F32
    )


def t_dot_full(left, right):
    return lax.dot_general(
        left, right, (((0,), (0,)), ((), ())), precision=HIGHEST, preferred_element_type=F32
    )


def two_parts(value):
    high = value.astype(BF16)
    return high, (value - high.astype(F32)).astype(BF16)


def dot_three(left, right, dims=((1,), (0,))):
    lh, ll = two_parts(left)
    rh, rl = two_parts(right)

    def one(a, b):
        return lax.dot_general(a, b, (dims, ((), ())), preferred_element_type=F32)

    return (one(lh, rl) + one(ll, rh)) + one(lh, rh)


def picks(start, count, total):
    row = lax.broadcasted_iota(jnp.int32, (count, total), 0)
    lane = lax.broadcasted_iota(jnp.int32, (count, total), 1)
    return jnp.where(lane - row == start, 1.0, 0.0).astype(BF16)


def places(start, count, total):
    row = lax.broadcasted_iota(jnp.int32, (total, count), 0)
    lane = lax.broadcasted_iota(jnp.int32, (total, count), 1)
    return jnp.where(row - lane == start, 1.0, 0.0).astype(BF16)


def three_parts(value):
    high = value.astype(BF16)
    rest = value - high.astype(F32)
    mid = rest.astype(BF16)
    return high, mid, (rest - mid.astype(F32)).astype(BF16)


def remote(src, dst, send_sem, recv_sem, w, c):
    return pltpu.make_async_remote_copy(
        src_ref=src,
        dst_ref=dst,
        send_sem=send_sem,
        recv_sem=recv_sem,
        device_id=(w, c),
        device_id_type=MESH,
    )


def greet(w, c, wide, col):
    barrier = pltpu.get_barrier_semaphore()

    def along_col(k, carry):
        pl.semaphore_signal(
            barrier, inc=1, device_id=(w, lax.rem(c + k, col)), device_id_type=MESH
        )
        return carry

    def along_wide(k, carry):
        pl.semaphore_signal(
            barrier, inc=1, device_id=(lax.rem(w + k, wide), c), device_id_type=MESH
        )
        return carry

    lax.fori_loop(1, col, along_col, 0)
    lax.fori_loop(1, wide, along_wide, 0)


def meet(wide, col):
    pl.semaphore_wait(pltpu.get_barrier_semaphore(), wide + col - 2)


def all_reduce(w, c, wide, col, g, half, land, ysl, out, send, recv):
    rows = g.shape[0]
    high = rows // 2
    part = high // col
    core = lax.rem(w, 2)
    y = w // 2
    ys = wide // 2
    partner = w + 1 - 2 * core
    mine = pl.multiple_of(core * high, high)
    other = pl.multiple_of((1 - core) * high, high)
    own = pl.multiple_of(mine + c * part, part)

    swap = remote(g.at[pl.ds(other, high)], half, send.at[0], recv.at[0], partner, c)
    swap.start()
    swap.wait()
    g[pl.ds(mine, high), :] += half[...]

    def scatter(k, carry):
        d = lax.rem(c + k, col)
        remote(
            g.at[pl.ds(pl.multiple_of(mine + d * part, part), part)],
            land.at[pl.ds(pl.multiple_of((col - 1 - k) * part, part), part)],
            send.at[1],
            recv.at[1],
            w,
            d,
        ).start()
        return carry

    lax.fori_loop(1, col, scatter, 0)
    many = (col - 1) * part
    remote(g.at[pl.ds(0, many)], land, send.at[1], recv.at[1], w, c).wait()
    total = g[pl.ds(own, part), :]
    for k in range(col - 1):
        total += land[k * part : (k + 1) * part, :]
    ysl[y] = total

    def spread(k, carry):
        other_y = lax.rem(y + k, ys)
        remote(ysl.at[y], ysl.at[y], send.at[2], recv.at[2], 2 * other_y + core, c).start()
        return carry

    lax.fori_loop(1, ys, spread, 0)
    few = pl.ds(0, ys - 1)
    remote(ysl.at[few], ysl.at[few], send.at[2], recv.at[2], w, c).wait()
    total = ysl[0]
    for k in range(1, ys):
        total += ysl[k]
    out[pl.ds(own, part), :] = total

    def gather(k, carry):
        d = lax.rem(c + k, col)
        spot = pl.ds(own, part)
        remote(out.at[spot], out.at[spot], send.at[3], recv.at[3], w, d).start()
        return carry

    lax.fori_loop(1, col, gather, 0)
    spot = pl.ds(0, many)
    remote(out.at[spot], out.at[spot], send.at[3], recv.at[3], w, c).wait()
    spot = pl.ds(mine, high)
    swap = remote(out.at[spot], out.at[spot], send.at[4], recv.at[4], partner, c)
    swap.start()
    swap.wait()


def reduce_scratch(rows, width, wide, col):
    high = rows // 2
    part = high // col
    return [
        pltpu.VMEM((rows, width), F32),
        pltpu.VMEM((high, width), F32),
        pltpu.VMEM(((col - 1) * part, width), F32),
        pltpu.VMEM((wide // 2, part, width), F32),
        pltpu.SemaphoreType.DMA((5,)),
        pltpu.SemaphoreType.DMA((5,)),
    ]


def local_grams(lefts, right, g, step):
    width = right.shape[1]
    rows = right.shape[0]
    for i, left in enumerate(lefts):
        spot = slice(i * width, (i + 1) * width)
        g[spot, :] = dot_three(left[0:step, :], right[0:step, :], ((0,), (0,)))

        def add(k, carry, left=left, spot=spot):
            piece = pl.ds(pl.multiple_of(k * step, step), step)
            g[spot, :] += dot_three(left[piece, :], right[piece, :], ((0,), (0,)))
            return carry

        lax.fori_loop(1, rows // step, add, 0)


def first_gram_kernel(wide, col, step, rhs, out, g, half, land, ysl, send, recv):
    w, c = lax.axis_index("wide"), lax.axis_index("col")
    greet(w, c, wide, col)
    local_grams([rhs], rhs, g, step)
    meet(wide, col)
    all_reduce(w, c, wide, col, g, half, land, ysl, out, send, recv)


def step_kernel(wide, col, step, first, *refs):
    if first:
        (starts, near_ids, order, x, mt, basis_h, self_h, near_h, coup_h, sch_h, *rest) = refs
        (v, z, wv, gram, *rest) = rest
    else:
        (starts, near_ids, order, x, mt, vprev, u, basis_h, self_h, near_h, coup_h, sch_h, *rest) = refs
        (z, gram, v, wv, *rest) = rest
    (basis, selfb, near, coup, sch, stage, dom, pad_next, pad_prev, edge, nb, win, far, *rest) = rest
    (load, hs, hr, ns, nr, ws, wr, rs, rr, ps, pr, *reduce) = rest
    g, half, land, ysl, send, recv = reduce
    w, c = lax.axis_index("wide"), lax.axis_index("col")
    core = lax.rem(w, 2)
    partner = w + 1 - 2 * core
    rows, width = x.shape
    margin = edge.shape[1]
    has_prev, has_next = c > 0, c < col - 1

    loads = [
        pltpu.make_async_copy(sch_h.at[0], sch, load.at[0]),
        pltpu.make_async_copy(basis_h, basis, load.at[1]),
        pltpu.make_async_copy(self_h, selfb, load.at[2]),
        pltpu.make_async_copy(near_h.at[0], near, load.at[3]),
        pltpu.make_async_copy(
            coup_h.at[0], coup.at[pl.ds(0, coup_h.shape[1])], load.at[4]
        ),
    ]
    for copy in loads:
        copy.start()

    @pl.when(jnp.logical_not(has_prev))
    def _():
        dom[0:margin, :] = jnp.zeros((margin, width), BF16)
        pad_prev[...] = jnp.zeros((margin, width), F32)

    @pl.when(jnp.logical_not(has_next))
    def _():
        dom[margin + rows :, :] = jnp.zeros((margin, width), BF16)
        pad_next[...] = jnp.zeros((margin, width), F32)

    for i in range(SPAN):
        for a in range(SPAN):
            dc, dw = i - REACH, a - REACH
            off = (w + dw < 0) | (w + dw >= wide) | (c + dc < 0) | (c + dc >= col)
            if (dw or dc) and max(abs(dw), abs(dc)) > 1:

                @pl.when(off)
                def _(cell=i * SPAN + a):
                    win[cell] = jnp.zeros(win.shape[1:], BF16)

    greet(w, c, wide, col)

    def make_v(k, carry):
        piece = pl.ds(pl.multiple_of(k * step, step), step)
        value = dot_full(x[piece, :], mt[...])
        if not first:
            value += dot_full(vprev[piece, :], u[...])
        v[piece, :] = value
        dom[pl.ds(pl.multiple_of(margin + k * step, step), step), :] = value.astype(BF16)
        return carry

    lax.fori_loop(0, rows // step, make_v, 0)
    start_prev, start_next = starts[0, 0], starts[0, 1]
    stage[0] = dot(picks(start_next, margin, rows), dom[margin : margin + rows, :]).astype(BF16)
    stage[1] = dot(picks(start_prev, margin, rows), dom[margin : margin + rows, :]).astype(BF16)
    meet(wide, col)

    to_next = remote(stage.at[0], dom.at[pl.ds(0, margin)], hs.at[0], hr.at[0], w, c + 1)
    to_prev = remote(
        stage.at[1], dom.at[pl.ds(margin + rows, margin)], hs.at[1], hr.at[1], w, c - 1
    )
    out_prev = remote(
        edge.at[0], pad_next, hs.at[2], hr.at[2], w, c - 1
    )
    out_next = remote(
        edge.at[1], pad_prev, hs.at[3], hr.at[3], w, c + 1
    )
    pl.when(has_next)(to_next.start)
    pl.when(has_prev)(to_prev.start)

    nb[9] = jnp.zeros((rows, width), BF16)

    loads[0].wait()
    pl.when(has_prev)(to_next.wait_recv)
    pl.when(has_next)(to_prev.wait_recv)
    edge[0] = dot(sch[0:margin, :], dom[...])
    pl.when(has_prev)(out_prev.start)
    edge[1] = dot(sch[margin + rows :, :], dom[...])
    pl.when(has_next)(out_next.start)

    def solve(k, carry):
        piece = pl.ds(pl.multiple_of(k * step, step), step)
        z[piece, :] = dot(sch[pl.ds(pl.multiple_of(margin + k * step, step), step), :], dom[...])
        return carry

    lax.fori_loop(0, rows // step, solve, 0)
    pl.when(has_next)(out_prev.wait_recv)
    pl.when(has_prev)(out_next.wait_recv)
    for start, pad in ((start_next, pad_next), (start_prev, pad_prev)):
        spread = places(start, margin, rows)
        for part in three_parts(pad[...]):
            z[...] += dot(spread, part)
    nb[4] = z[...].astype(BF16)
    loads[1].wait()

    def near_to(dw, dc, source):
        return remote(
            nb.at[source], nb.at[(1 - dw) * 3 + dc + 1], ns.at[(1 - dw) * 3 + dc + 1],
            nr.at[(1 - dw) * 3 + dc + 1], w + dw, c,
        )

    def near_col(dc):
        return remote(nb.at[4], nb.at[4 - dc], ns.at[4 - dc], nr.at[4 - dc], w, c + dc)

    beside = {-1: has_prev, 1: has_next}
    within = {d: (w + d >= 0) & (w + d < wide) for d in range(-REACH, REACH + 1) if d}
    for d in (-1, 1):
        pl.when(beside[d])(near_col(d).start)
    for d in (-1, 1):
        pl.when(within[d])(near_to(d, 0, 4).start)

    centre = REACH * SPAN + REACH
    win[centre] = lax.dot_general(
        basis[...], nb[4], (((0,), (0,)), ((), ())), preferred_element_type=F32
    ).astype(BF16)

    def far_wide(d):
        return remote(
            win.at[centre], win.at[centre - d], ws.at[REACH - d], wr.at[REACH - d], w + d, c
        )

    for d in (1, -1, 2, -2, 3, -3):
        pl.when(within[d])(far_wide(d).start)

    def on_grid(a):
        return (w + a - REACH >= 0) & (w + a - REACH < wide)

    def hand_on(direction, k, j):
        held = REACH - direction * (k - 1)
        lands = held - direction
        a = REACH * core + j
        return remote(
            win.at[held * SPAN + a], win.at[lands * SPAN + a],
            rs.at[lands * (REACH + 1) + j], rr.at[lands * (REACH + 1) + j], w, c + direction,
        )

    def share(i, j):
        return remote(
            win.at[i * SPAN + 1 + 2 * core + j], win.at[i * SPAN + (REACH + 1) * core + j],
            ps.at[i * REACH + j], pr.at[i * REACH + j], partner, c,
        )

    def arrives(direction, k):
        return c - k >= 0 if direction > 0 else c + k < col

    def sends(direction, k):
        held = c - (k - 1) >= 0 if direction > 0 else c + (k - 1) < col
        return held & beside[direction]

    def each(count, body):
        def run(j, carry):
            body(j)
            return carry

        lax.fori_loop(0, count, run, 0)

    def pass_on(direction, k):
        def row(j):
            here = arrives(direction, k) & on_grid(REACH * core + j)

            @pl.when(here)
            def _():
                hand_on(direction, k, j).wait_recv()

            if k < REACH:
                @pl.when(sends(direction, k + 1) & on_grid(REACH * core + j))
                def _():
                    hand_on(direction, k + 1, j).start()

        each(REACH + 1, row)
        i = REACH - direction * k

        def across(j):
            @pl.when(arrives(direction, k) & on_grid(1 + 2 * core + j))
            def _():
                share(i, j).start()

        each(REACH, across)

    def take_share(direction, k):
        i = REACH - direction * k

        def row(j):
            @pl.when(arrives(direction, k) & on_grid((REACH + 1) * (1 - core) + j))
            def _():
                share(i, j).wait_recv()

        each(REACH, row)

    def far_strip(i):
        total = None
        for a in range(SPAN):
            if abs(i - REACH) > 1 or abs(a - REACH) > 1:
                term = dot(coup[order[0, i * SPAN + a]], win[i * SPAN + a])
                total = term if total is None else total + term
        far[...] += total

    for d in within:
        pl.when(within[-d])(far_wide(d).wait_recv)

    def first_hand(j):
        for d in (1, -1):
            @pl.when(beside[d] & on_grid(REACH * core + j))
            def _(d=d):
                hand_on(d, 1, j).start()

    each(REACH + 1, first_hand)

    loads[2].wait()
    wv[...] = dot(selfb[...], nb[4])

    for d in (-1, 1):
        pl.when(beside[d])(near_col(-d).wait_recv)
        for e in (-1, 1):
            pl.when(beside[d] & within[e])(near_to(e, d, 4 + d).start)

    loads[4].wait()
    coup[coup.shape[0] - 1] = jnp.zeros(coup.shape[1:], BF16)
    far[...] = jnp.zeros_like(far)
    far_strip(REACH)
    for d in (1, -1):
        pass_on(d, 1)
    for d in (1, -1):
        take_share(d, 1)
    far_strip(REACH - 1)
    far_strip(REACH + 1)
    for d in (1, -1):
        pass_on(d, 2)

    for e in (-1, 1):
        for d in (-1, 0, 1):
            ok = within[-e] if d == 0 else within[-e] & beside[d]
            pl.when(ok)(near_to(e, d, 4 + d).wait_recv)
    loads[3].wait()

    def near_slot(s, carry):
        cluster = near_ids[0, s]
        place = (lax.div(cluster, col) - w + 1) * 3 + (lax.rem(cluster, col) - c + 1)
        place = jnp.where(cluster >= 0, jnp.minimum(jnp.maximum(place, 0), 8), 9)
        wv[...] += dot(near[s], nb[place])
        return carry

    lax.fori_loop(0, near_ids.shape[1], near_slot, 0)
    for d in (1, -1):
        pass_on(d, 3)
    for d in (1, -1):
        take_share(d, 2)
    far_strip(REACH - 2)
    far_strip(REACH + 2)
    for d in (1, -1):
        take_share(d, 3)
    far_strip(REACH - 3)
    far_strip(REACH + 3)
    wv[...] += dot(basis[...], far[...].astype(BF16))
    local_grams([v, wv] if first else [vprev, x, wv], wv, g, step)

    pl.when(has_next)(to_next.wait_send)
    pl.when(has_prev)(to_prev.wait_send)
    pl.when(has_prev)(out_prev.wait_send)
    pl.when(has_next)(out_next.wait_send)
    for d in (-1, 1):
        pl.when(beside[d])(near_col(d).wait_send)
        pl.when(within[d])(near_to(d, 0, 4).wait_send)
        for e in (-1, 1):
            pl.when(beside[d] & within[e])(near_to(e, d, 4 + d).wait_send)
    for d in within:
        pl.when(within[d])(far_wide(d).wait_send)
    for k in range(1, REACH + 1):
        for d in (1, -1):

            def sent(j, d=d, k=k):
                @pl.when(sends(d, k) & on_grid(REACH * core + j))
                def _():
                    hand_on(d, k, j).wait_send()

            def shared(j, d=d, k=k):
                @pl.when(arrives(d, k) & on_grid(1 + 2 * core + j))
                def _():
                    share(REACH - d * k, j).wait_send()

            each(REACH + 1, sent)
            each(REACH, shared)

    all_reduce(w, c, wide, col, g, half, land, ysl, gram, send, recv)


def inverse_factors(matrices, scratch):
    n = matrices[0].shape[0]
    row = lax.broadcasted_iota(jnp.int32, (n, n), 0)
    lane = lax.broadcasted_iota(jnp.int32, (n, n), 1)
    eye = (row == lane).astype(F32)

    def lower(e):
        return jnp.where(row > lane, e, 0.5 * e * eye)

    scaled, scales = [], []
    for i, a in enumerate(matrices):
        only = a * eye
        by_row = lax.rsqrt(jnp.sum(only, axis=1, keepdims=True))
        by_lane = lax.rsqrt(jnp.sum(only, axis=0, keepdims=True))
        a = a * by_row * by_lane
        scratch[i] = eye - lower(a - eye)
        scaled.append(a)
        scales.append(by_lane)
    limit = 1e-5

    def go_on(state):
        step, error = state
        return (step < 8) & jnp.logical_not(error < limit)

    def refine(state):
        step, _ = state
        error = jnp.float32(0.0)
        for i, a in enumerate(scaled):
            m = scratch[i]
            e = dot_full_t(dot_full(m, a), m) - eye
            scratch[i] = m - dot_three(lower(e), m)
            error = error + jnp.sum(e * e)
        return step + 1, error

    _, error = lax.while_loop(go_on, refine, (jnp.int32(0), jnp.float32(1.0)))

    @pl.when(jnp.logical_not(error < limit))
    def _():
        for i, a in enumerate(scaled):

            def eliminate(j, state):
                s, m = state
                at_lane = jnp.sum(jnp.where(lane == j, s, 0.0), axis=1, keepdims=True)
                at_row = jnp.sum(jnp.where(row == j, s, 0.0), axis=0, keepdims=True)
                m_row = jnp.sum(jnp.where(row == j, m, 0.0), axis=0, keepdims=True)
                pivot = jnp.sum(jnp.where(row == j, at_lane, 0.0), axis=0, keepdims=True)
                pivot = pivot[:, 0:1]
                times = jnp.where(row[:, 0:1] > j, at_lane / pivot, 0.0)
                s = s - times * at_row
                m = m - times * m_row
                m = jnp.where(row == j, m_row * lax.rsqrt(pivot), m)
                return s, m

            _, m = lax.fori_loop(0, n, eliminate, (a, eye))
            scratch[i] = m

    for i, by_lane in enumerate(scales):
        scratch[i] = scratch[i] * by_lane


def first_factor_kernel(col, far_ids, g0, m, mt, order):
    w, c = lax.axis_index("wide"), lax.axis_index("col")
    slots = far_ids.shape[1]

    def clear(p, carry):
        order[0, p] = slots
        return carry

    def put(s, carry):
        cluster = far_ids[0, s]

        @pl.when(cluster >= 0)
        def _():
            dc = lax.rem(cluster, col) - c + REACH
            dw = lax.div(cluster, col) - w + REACH
            order[0, dc * SPAN + dw] = s

        return carry

    lax.fori_loop(0, SPAN * SPAN, clear, 0)
    lax.fori_loop(0, slots, put, 0)
    inverse_factors([g0[...]], m)
    mt[...] = m[0].T


def second_factor_kernel(gram, m, mt, u):
    k = gram.shape[1]
    h = gram[0:k, :]
    n = gram[k:, :]
    inverse_factors([n - t_dot_full(h, h), n], m)
    mt[...] = m[0].T
    u[...] = -dot_full(h, mt[...])


def last_kernel(step, g0, m0, gram1, mn, gram2, z1, z2, out, m):
    k = g0.shape[1]
    down = ((0,), (0,))
    beta = dot_three(m0[0], g0[...])
    h1, h2 = gram1[0:k, :], gram2[0:k, :]
    n12, n22 = gram2[k : 2 * k, :], gram2[2 * k :, :]
    first = mn[1]
    b1 = dot_three(first, dot_three(h1, beta, down))
    t = dot_full(first, n12)
    inverse_factors([n22 - t_dot_full(t, t)], m)
    b2 = dot_three(h2, beta, down) - dot_three(t, b1, down)
    y2 = dot_three(m[0], dot_three(m[0], b2), down)
    y1 = dot_three(first, b1 - dot_three(t, y2), down)

    def combine(i, carry):
        piece = pl.ds(pl.multiple_of(i * step, step), step)
        out[piece, :] = dot_three(z1[piece, :], y1) + dot_three(z2[piece, :], y2)
        return carry

    lax.fori_loop(0, out.shape[0] // step, combine, 0)


def on_device(
    wide, col, rhs, basis, self_block, near_block, near_ids, couplings, far_ids, starts, schwarz_inverse
):
    rows, width = rhs.shape
    rank = basis.shape[1]
    order = schwarz_inverse.shape[1]
    margin = (order - rows) // 2
    step = rows // 3
    slots, links = near_ids.shape[1], far_ids.shape[1]
    vmem = pl.BlockSpec(memory_space=pltpu.VMEM)
    smem = pl.BlockSpec(memory_space=pltpu.SMEM)
    anywhere = pl.BlockSpec(memory_space=pl.ANY)

    def block(n):
        return jax.ShapeDtypeStruct((n, width), F32)

    square = jax.ShapeDtypeStruct((1, width, width), F32)
    local = pltpu.CompilerParams(vmem_limit_bytes=VMEM_BYTES)

    def talks(number):
        return pltpu.CompilerParams(
            collective_id=number, has_side_effects=True, vmem_limit_bytes=VMEM_BYTES
        )

    gram0 = pl.pallas_call(
        functools.partial(first_gram_kernel, wide, col, step),
        out_shape=block(width),
        in_specs=[vmem],
        out_specs=vmem,
        scratch_shapes=reduce_scratch(width, width, wide, col),
        compiler_params=talks(0),
        name="first_gram",
    )(rhs)
    m0, mt0, listed = pl.pallas_call(
        functools.partial(first_factor_kernel, col),
        out_shape=(square, block(width), jax.ShapeDtypeStruct((1, SPAN * SPAN), jnp.int32)),
        in_specs=[smem, vmem],
        out_specs=(vmem, vmem, smem),
        compiler_params=local,
        name="first_factor",
    )(far_ids, gram0)

    def take_step(first, *blocks):
        grams = 2 if first else 3
        outs = [block(rows)] * 3 if first else [block(rows)]
        held = [] if first else [pltpu.VMEM((rows, width), F32)] * 2
        dma = pltpu.SemaphoreType.DMA
        return pl.pallas_call(
            functools.partial(step_kernel, wide, col, step, first),
            out_shape=(*outs, block(grams * width)),
            in_specs=[smem] * 3 + [vmem] * len(blocks) + [anywhere] * 5,
            out_specs=(vmem,) * (len(outs) + 1),
            scratch_shapes=held
            + [
                pltpu.VMEM((rows, rank), BF16),
                pltpu.VMEM((rows, rows), BF16),
                pltpu.VMEM((slots, rows, rows), BF16),
                pltpu.VMEM((links + 1, rank, rank), BF16),
                pltpu.VMEM((order, order), BF16),
                pltpu.VMEM((2, margin, width), BF16),
                pltpu.VMEM((order, width), BF16),
                pltpu.VMEM((margin, width), F32),
                pltpu.VMEM((margin, width), F32),
                pltpu.VMEM((2, margin, width), F32),
                pltpu.VMEM((10, rows, width), BF16),
                pltpu.VMEM((SPAN * SPAN, rank, width), BF16),
                pltpu.VMEM((rank, width), F32),
                dma((5,)),
                dma((4,)),
                dma((4,)),
                dma((9,)),
                dma((9,)),
                dma((SPAN,)),
                dma((SPAN,)),
                dma((SPAN * (REACH + 1),)),
                dma((SPAN * (REACH + 1),)),
                dma((SPAN * REACH,)),
                dma((SPAN * REACH,)),
            ]
            + reduce_scratch(grams * width, width, wide, col),
            compiler_params=talks(1 if first else 2),
            name="first_step" if first else "second_step",
        )(starts, near_ids, listed, *blocks, basis, self_block, near_block, couplings, schwarz_inverse)

    v1, z1, w1, gram1 = take_step(True, rhs, mt0)
    m1, mt1, u = pl.pallas_call(
        second_factor_kernel,
        out_shape=(jax.ShapeDtypeStruct((2, width, width), F32), block(width), block(width)),
        in_specs=[vmem],
        out_specs=(vmem,) * 3,
        compiler_params=local,
        name="second_factor",
    )(gram1)
    z2, gram2 = take_step(False, w1, mt1, v1, u)
    return pl.pallas_call(
        functools.partial(last_kernel, step),
        out_shape=block(rows),
        in_specs=[vmem] * 7,
        out_specs=vmem,
        scratch_shapes=[pltpu.VMEM((1, width, width), F32)],
        compiler_params=local,
        name="last",
    )(gram0, m0, gram1, m1, gram2, z1, z2)


def solution(mesh):
    in_specs = (
        P(("wide", "col"), None),
        P(("wide", "col"), None),
        P(("wide", "col"), None),
        P(("wide", "col"), None, None, None),
        P(("wide", "col"), None),
        P(("wide", "col"), None, None, None),
        P(("wide", "col"), None),
        P(("wide", "col"), None),
        P(("wide", "col"), None, None),
    )
    out_specs = P(("wide", "col"), None)
    return jax.shard_map(
        functools.partial(on_device, mesh.shape["wide"], mesh.shape["col"]),
        mesh=mesh,
        in_specs=in_specs,
        out_specs=out_specs,
        check_vma=False,
    )
```

```python
import functools

import jax
import jax.numpy as jnp
from jax import lax
from jax.experimental import pallas as pl
from jax.experimental.pallas import tpu as pltpu
from jax.sharding import PartitionSpec as P

REACH = 3
SPAN = 2 * REACH + 1
MESH = pl.DeviceIdType.MESH
HIGHEST = lax.Precision.HIGHEST
F32 = jnp.float32
BF16 = jnp.bfloat16
VMEM_BYTES = 60 * 1024 * 1024


def dot(left, right):
    return jnp.dot(left, right, preferred_element_type=F32)


def dot_full(left, right):
    return jnp.dot(left, right, precision=HIGHEST, preferred_element_type=F32)


def dot_full_t(left, right):
    return lax.dot_general(
        left, right, (((1,), (1,)), ((), ())), precision=HIGHEST, preferred_element_type=F32
    )


def t_dot_full(left, right):
    return lax.dot_general(
        left, right, (((0,), (0,)), ((), ())), precision=HIGHEST, preferred_element_type=F32
    )


def two_parts(value):
    high = value.astype(BF16)
    return high, (value - high.astype(F32)).astype(BF16)


def dot_three(left, right, dims=((1,), (0,))):
    lh, ll = two_parts(left)
    rh, rl = two_parts(right)

    def one(a, b):
        return lax.dot_general(a, b, (dims, ((), ())), preferred_element_type=F32)

    return (one(lh, rl) + one(ll, rh)) + one(lh, rh)


def picks(start, count, total):
    row = lax.broadcasted_iota(jnp.int32, (count, total), 0)
    lane = lax.broadcasted_iota(jnp.int32, (count, total), 1)
    return jnp.where(lane - row == start, 1.0, 0.0).astype(BF16)


def places(start, count, total):
    row = lax.broadcasted_iota(jnp.int32, (total, count), 0)
    lane = lax.broadcasted_iota(jnp.int32, (total, count), 1)
    return jnp.where(row - lane == start, 1.0, 0.0).astype(BF16)


def three_parts(value):
    high = value.astype(BF16)
    rest = value - high.astype(F32)
    mid = rest.astype(BF16)
    return high, mid, (rest - mid.astype(F32)).astype(BF16)


def remote(src, dst, send_sem, recv_sem, w, c):
    return pltpu.make_async_remote_copy(
        src_ref=src,
        dst_ref=dst,
        send_sem=send_sem,
        recv_sem=recv_sem,
        device_id=(w, c),
        device_id_type=MESH,
    )


def greet(w, c, wide, col):
    barrier = pltpu.get_barrier_semaphore()

    def along_col(k, carry):
        pl.semaphore_signal(
            barrier, inc=1, device_id=(w, lax.rem(c + k, col)), device_id_type=MESH
        )
        return carry

    def along_wide(k, carry):
        pl.semaphore_signal(
            barrier, inc=1, device_id=(lax.rem(w + k, wide), c), device_id_type=MESH
        )
        return carry

    lax.fori_loop(1, col, along_col, 0)
    lax.fori_loop(1, wide, along_wide, 0)


def meet(wide, col):
    pl.semaphore_wait(pltpu.get_barrier_semaphore(), wide + col - 2)


def all_reduce(w, c, wide, col, g, half, land, ysl, out, send, recv):
    rows = g.shape[0]
    high = rows // 2
    part = high // col
    core = lax.rem(w, 2)
    y = w // 2
    ys = wide // 2
    partner = w + 1 - 2 * core
    mine = pl.multiple_of(core * high, high)
    other = pl.multiple_of((1 - core) * high, high)
    own = pl.multiple_of(mine + c * part, part)

    swap = remote(g.at[pl.ds(other, high)], half, send.at[0], recv.at[0], partner, c)
    swap.start()
    swap.wait()
    g[pl.ds(mine, high), :] += half[...]

    def scatter(k, carry):
        d = lax.rem(c + k, col)
        remote(
            g.at[pl.ds(pl.multiple_of(mine + d * part, part), part)],
            land.at[pl.ds(pl.multiple_of((col - 1 - k) * part, part), part)],
            send.at[1],
            recv.at[1],
            w,
            d,
        ).start()
        return carry

    lax.fori_loop(1, col, scatter, 0)
    many = (col - 1) * part
    remote(g.at[pl.ds(0, many)], land, send.at[1], recv.at[1], w, c).wait()
    total = g[pl.ds(own, part), :]
    for k in range(col - 1):
        total += land[k * part : (k + 1) * part, :]
    ysl[y] = total

    def spread(k, carry):
        other_y = lax.rem(y + k, ys)
        remote(ysl.at[y], ysl.at[y], send.at[2], recv.at[2], 2 * other_y + core, c).start()
        return carry

    lax.fori_loop(1, ys, spread, 0)
    few = pl.ds(0, ys - 1)
    remote(ysl.at[few], ysl.at[few], send.at[2], recv.at[2], w, c).wait()
    total = ysl[0]
    for k in range(1, ys):
        total += ysl[k]
    out[pl.ds(own, part), :] = total

    def gather(k, carry):
        d = lax.rem(c + k, col)
        spot = pl.ds(own, part)
        remote(out.at[spot], out.at[spot], send.at[3], recv.at[3], w, d).start()
        return carry

    lax.fori_loop(1, col, gather, 0)
    spot = pl.ds(0, many)
    remote(out.at[spot], out.at[spot], send.at[3], recv.at[3], w, c).wait()
    spot = pl.ds(mine, high)
    swap = remote(out.at[spot], out.at[spot], send.at[4], recv.at[4], partner, c)
    swap.start()
    swap.wait()


def reduce_scratch(rows, width, wide, col):
    high = rows // 2
    part = high // col
    return [
        pltpu.VMEM((rows, width), F32),
        pltpu.VMEM((high, width), F32),
        pltpu.VMEM(((col - 1) * part, width), F32),
        pltpu.VMEM((wide // 2, part, width), F32),
        pltpu.SemaphoreType.DMA((5,)),
        pltpu.SemaphoreType.DMA((5,)),
    ]


def local_grams(lefts, right, g, step):
    width = right.shape[1]
    rows = right.shape[0]
    for i, left in enumerate(lefts):
        spot = slice(i * width, (i + 1) * width)
        g[spot, :] = dot_three(left[0:step, :], right[0:step, :], ((0,), (0,)))

        def add(k, carry, left=left, spot=spot):
            piece = pl.ds(pl.multiple_of(k * step, step), step)
            g[spot, :] += dot_three(left[piece, :], right[piece, :], ((0,), (0,)))
            return carry

        lax.fori_loop(1, rows // step, add, 0)


def first_gram_kernel(wide, col, step, rhs, out, g, half, land, ysl, send, recv):
    w, c = lax.axis_index("wide"), lax.axis_index("col")
    greet(w, c, wide, col)
    local_grams([rhs], rhs, g, step)
    meet(wide, col)
    all_reduce(w, c, wide, col, g, half, land, ysl, out, send, recv)


def step_kernel(wide, col, step, first, *refs):
    if first:
        (starts, near_ids, order, x, mt, basis_h, self_h, near_h, coup_h, sch_h, *rest) = refs
        (v, z, wv, gram, *rest) = rest
    else:
        (starts, near_ids, order, x, mt, vprev, u, basis_h, self_h, near_h, coup_h, sch_h, *rest) = refs
        (z, gram, v, wv, *rest) = rest
    (basis, selfb, near, coup, sch, stage, dom, pad_next, pad_prev, edge, nb, win, far, *rest) = rest
    (load, hs, hr, ns, nr, ws, wr, rs, rr, es, ps, pr, *reduce) = rest
    g, half, land, ysl, send, recv = reduce
    w, c = lax.axis_index("wide"), lax.axis_index("col")
    core = lax.rem(w, 2)
    partner = w + 1 - 2 * core
    rows, width = x.shape
    margin = edge.shape[1]
    has_prev, has_next = c > 0, c < col - 1

    loads = [
        pltpu.make_async_copy(sch_h.at[0], sch, load.at[0]),
        pltpu.make_async_copy(basis_h, basis, load.at[1]),
        pltpu.make_async_copy(self_h, selfb, load.at[2]),
        pltpu.make_async_copy(near_h.at[0], near, load.at[3]),
        pltpu.make_async_copy(
            coup_h.at[0], coup.at[pl.ds(0, coup_h.shape[1])], load.at[4]
        ),
    ]
    for copy in loads:
        copy.start()

    @pl.when(jnp.logical_not(has_prev))
    def _():
        dom[0:margin, :] = jnp.zeros((margin, width), BF16)
        pad_prev[...] = jnp.zeros((margin, width), F32)

    @pl.when(jnp.logical_not(has_next))
    def _():
        dom[margin + rows :, :] = jnp.zeros((margin, width), BF16)
        pad_next[...] = jnp.zeros((margin, width), F32)

    for i in range(SPAN):
        for a in range(SPAN):
            dc, dw = i - REACH, a - REACH
            off = (w + dw < 0) | (w + dw >= wide) | (c + dc < 0) | (c + dc >= col)
            if (dw or dc) and max(abs(dw), abs(dc)) > 1:

                @pl.when(off)
                def _(cell=i * SPAN + a):
                    win[cell] = jnp.zeros(win.shape[1:], BF16)

    greet(w, c, wide, col)

    def make_v(k, carry):
        piece = pl.ds(pl.multiple_of(k * step, step), step)
        value = dot_full(x[piece, :], mt[...])
        if not first:
            value += dot_full(vprev[piece, :], u[...])
        v[piece, :] = value
        dom[pl.ds(pl.multiple_of(margin + k * step, step), step), :] = value.astype(BF16)
        return carry

    lax.fori_loop(0, rows // step, make_v, 0)
    start_prev, start_next = starts[0, 0], starts[0, 1]
    stage[0] = dot(picks(start_next, margin, rows), dom[margin : margin + rows, :]).astype(BF16)
    stage[1] = dot(picks(start_prev, margin, rows), dom[margin : margin + rows, :]).astype(BF16)
    meet(wide, col)

    to_next = remote(stage.at[0], dom.at[pl.ds(0, margin)], hs.at[0], hr.at[0], w, c + 1)
    to_prev = remote(
        stage.at[1], dom.at[pl.ds(margin + rows, margin)], hs.at[1], hr.at[1], w, c - 1
    )
    out_prev = remote(
        edge.at[0], pad_next, hs.at[2], hr.at[2], w, c - 1
    )
    out_next = remote(
        edge.at[1], pad_prev, hs.at[3], hr.at[3], w, c + 1
    )
    pl.when(has_next)(to_next.start)
    pl.when(has_prev)(to_prev.start)

    nb[9] = jnp.zeros((rows, width), BF16)

    loads[0].wait()
    pl.when(has_prev)(to_next.wait_recv)
    pl.when(has_next)(to_prev.wait_recv)
    edge[0] = dot(sch[0:margin, :], dom[...])
    pl.when(has_prev)(out_prev.start)
    edge[1] = dot(sch[margin + rows :, :], dom[...])
    pl.when(has_next)(out_next.start)

    def solve(k, carry):
        piece = pl.ds(pl.multiple_of(k * step, step), step)
        z[piece, :] = dot(sch[pl.ds(pl.multiple_of(margin + k * step, step), step), :], dom[...])
        return carry

    lax.fori_loop(0, rows // step, solve, 0)
    pl.when(has_next)(out_prev.wait_recv)
    pl.when(has_prev)(out_next.wait_recv)
    for start, pad in ((start_next, pad_next), (start_prev, pad_prev)):
        spread = places(start, margin, rows)
        for part in three_parts(pad[...]):
            z[...] += dot(spread, part)
    nb[4] = z[...].astype(BF16)
    loads[1].wait()

    def near_to(dw, dc, source):
        return remote(
            nb.at[source], nb.at[(1 - dw) * 3 + dc + 1], ns.at[(1 - dw) * 3 + dc + 1],
            nr.at[(1 - dw) * 3 + dc + 1], w + dw, c,
        )

    def near_col(dc):
        return remote(nb.at[4], nb.at[4 - dc], ns.at[4 - dc], nr.at[4 - dc], w, c + dc)

    beside = {-1: has_prev, 1: has_next}
    within = {d: (w + d >= 0) & (w + d < wide) for d in range(-REACH, REACH + 1) if d}
    for d in (-1, 1):
        pl.when(beside[d])(near_col(d).start)
    for d in (-1, 1):
        pl.when(within[d])(near_to(d, 0, 4).start)

    centre = REACH * SPAN + REACH
    win[centre] = lax.dot_general(
        basis[...], nb[4], (((0,), (0,)), ((), ())), preferred_element_type=F32
    ).astype(BF16)

    def far_wide(d):
        return remote(
            win.at[centre], win.at[centre - d], ws.at[REACH - d], wr.at[REACH - d], w + d, c
        )

    for d in (1, -1, 2, -2, 3, -3):
        pl.when(within[d])(far_wide(d).start)

    def on_grid(a):
        return (w + a - REACH >= 0) & (w + a - REACH < wide)

    def hand_on(direction, k, j):
        held = REACH - direction * (k - 1)
        lands = held - direction
        a = REACH * core + j
        return remote(
            win.at[held * SPAN + a], win.at[lands * SPAN + a],
            rs.at[lands * (REACH + 1) + j], rr.at[lands * (REACH + 1) + j], w, c + direction,
        )

    def jump(direction, j):
        lands = REACH - direction * REACH
        a = REACH * core + j
        return remote(
            win.at[(REACH + direction) * SPAN + a], win.at[lands * SPAN + a],
            rs.at[lands * (REACH + 1) + j], rr.at[lands * (REACH + 1) + j],
            w, c + direction * (REACH + 1),
        )

    def jumps(direction):
        return c + REACH + 1 < col if direction > 0 else c - REACH - 1 >= 0

    def from_end(direction, j):
        lands = REACH - direction * REACH
        a = REACH * core + j
        return remote(
            win.at[REACH * SPAN + a], win.at[lands * SPAN + a],
            es.at[lands * (REACH + 1) + j], rr.at[lands * (REACH + 1) + j],
            w, c + direction * REACH,
        )

    def at_end(direction):
        if direction > 0:
            return (c == 0) & (c + REACH < col)
        return (c == col - 1) & (c - REACH >= 0)

    def share(i, j):
        return remote(
            win.at[i * SPAN + 1 + 2 * core + j], win.at[i * SPAN + (REACH + 1) * core + j],
            ps.at[i * REACH + j], pr.at[i * REACH + j], partner, c,
        )

    def arrives(direction, k):
        return c - k >= 0 if direction > 0 else c + k < col

    def sends(direction, k):
        held = c - (k - 1) >= 0 if direction > 0 else c + (k - 1) < col
        return held & beside[direction]

    def each(count, body):
        def run(j, carry):
            body(j)
            return carry

        lax.fori_loop(0, count, run, 0)

    def pass_on(direction, k):
        def row(j):
            here = arrives(direction, k) & on_grid(REACH * core + j)

            @pl.when(here)
            def _():
                hand_on(direction, k, j).wait_recv()

            if k == 1:
                @pl.when(here & jumps(-direction))
                def _():
                    jump(-direction, j).start()

            if k + 1 < REACH:
                @pl.when(sends(direction, k + 1) & on_grid(REACH * core + j))
                def _():
                    hand_on(direction, k + 1, j).start()

        each(REACH + 1, row)
        i = REACH - direction * k

        def across(j):
            @pl.when(arrives(direction, k) & on_grid(1 + 2 * core + j))
            def _():
                share(i, j).start()

        each(REACH, across)

    def take_share(direction, k):
        i = REACH - direction * k

        def row(j):
            @pl.when(arrives(direction, k) & on_grid((REACH + 1) * (1 - core) + j))
            def _():
                share(i, j).wait_recv()

        each(REACH, row)

    def far_strip(i):
        total = None
        for a in range(SPAN):
            if abs(i - REACH) > 1 or abs(a - REACH) > 1:
                term = dot(coup[order[0, i * SPAN + a]], win[i * SPAN + a])
                total = term if total is None else total + term
        far[...] += total

    for d in within:
        pl.when(within[-d])(far_wide(d).wait_recv)

    def first_hand(j):
        for d in (1, -1):
            @pl.when(beside[d] & on_grid(REACH * core + j))
            def _(d=d):
                hand_on(d, 1, j).start()

            @pl.when(at_end(d) & on_grid(REACH * core + j))
            def _(d=d):
                from_end(d, j).start()

    each(REACH + 1, first_hand)

    loads[2].wait()
    wv[...] = dot(selfb[...], nb[4])

    for d in (-1, 1):
        pl.when(beside[d])(near_col(-d).wait_recv)
        for e in (-1, 1):
            pl.when(beside[d] & within[e])(near_to(e, d, 4 + d).start)

    loads[4].wait()
    coup[coup.shape[0] - 1] = jnp.zeros(coup.shape[1:], BF16)
    far[...] = jnp.zeros_like(far)
    far_strip(REACH)
    for d in (1, -1):
        pass_on(d, 1)
    for d in (1, -1):
        take_share(d, 1)
    far_strip(REACH - 1)
    far_strip(REACH + 1)
    for d in (1, -1):
        pass_on(d, 2)

    for e in (-1, 1):
        for d in (-1, 0, 1):
            ok = within[-e] if d == 0 else within[-e] & beside[d]
            pl.when(ok)(near_to(e, d, 4 + d).wait_recv)
    loads[3].wait()

    def near_slot(s, carry):
        cluster = near_ids[0, s]
        place = (lax.div(cluster, col) - w + 1) * 3 + (lax.rem(cluster, col) - c + 1)
        place = jnp.where(cluster >= 0, jnp.minimum(jnp.maximum(place, 0), 8), 9)
        wv[...] += dot(near[s], nb[place])
        return carry

    lax.fori_loop(0, near_ids.shape[1], near_slot, 0)
    for d in (1, -1):
        pass_on(d, 3)
    for d in (1, -1):
        take_share(d, 2)
    far_strip(REACH - 2)
    far_strip(REACH + 2)
    for d in (1, -1):
        take_share(d, 3)
    far_strip(REACH - 3)
    far_strip(REACH + 3)
    wv[...] += dot(basis[...], far[...].astype(BF16))
    local_grams([v, wv] if first else [vprev, x, wv], wv, g, step)

    pl.when(has_next)(to_next.wait_send)
    pl.when(has_prev)(to_prev.wait_send)
    pl.when(has_prev)(out_prev.wait_send)
    pl.when(has_next)(out_next.wait_send)
    for d in (-1, 1):
        pl.when(beside[d])(near_col(d).wait_send)
        pl.when(within[d])(near_to(d, 0, 4).wait_send)
        for e in (-1, 1):
            pl.when(beside[d] & within[e])(near_to(e, d, 4 + d).wait_send)
    for d in within:
        pl.when(within[d])(far_wide(d).wait_send)
    for k in range(1, REACH + 1):
        for d in (1, -1):

            def sent(j, d=d, k=k):
                if k < REACH:
                    @pl.when(sends(d, k) & on_grid(REACH * core + j))
                    def _():
                        hand_on(d, k, j).wait_send()
                else:
                    @pl.when(arrives(-d, 1) & jumps(d) & on_grid(REACH * core + j))
                    def _():
                        jump(d, j).wait_send()

                    @pl.when(at_end(d) & on_grid(REACH * core + j))
                    def _():
                        from_end(d, j).wait_send()

            def shared(j, d=d, k=k):
                @pl.when(arrives(d, k) & on_grid(1 + 2 * core + j))
                def _():
                    share(REACH - d * k, j).wait_send()

            each(REACH + 1, sent)
            each(REACH, shared)

    all_reduce(w, c, wide, col, g, half, land, ysl, gram, send, recv)


def inverse_factors(matrices, scratch):
    n = matrices[0].shape[0]
    row = lax.broadcasted_iota(jnp.int32, (n, n), 0)
    lane = lax.broadcasted_iota(jnp.int32, (n, n), 1)
    eye = (row == lane).astype(F32)

    def lower(e):
        return jnp.where(row > lane, e, 0.5 * e * eye)

    scaled, scales = [], []
    for i, a in enumerate(matrices):
        only = a * eye
        by_row = lax.rsqrt(jnp.sum(only, axis=1, keepdims=True))
        by_lane = lax.rsqrt(jnp.sum(only, axis=0, keepdims=True))
        a = a * by_row * by_lane
        scratch[i] = eye - lower(a - eye)
        scaled.append(a)
        scales.append(by_lane)
    limit = 1e-5

    def go_on(state):
        step, error = state
        return (step < 8) & jnp.logical_not(error < limit)

    def refine(state):
        step, _ = state
        error = jnp.float32(0.0)
        for i, a in enumerate(scaled):
            m = scratch[i]
            e = dot_full_t(dot_full(m, a), m) - eye
            scratch[i] = m - dot_three(lower(e), m)
            error = error + jnp.sum(e * e)
        return step + 1, error

    _, error = lax.while_loop(go_on, refine, (jnp.int32(0), jnp.float32(1.0)))

    @pl.when(jnp.logical_not(error < limit))
    def _():
        for i, a in enumerate(scaled):

            def eliminate(j, state):
                s, m = state
                at_lane = jnp.sum(jnp.where(lane == j, s, 0.0), axis=1, keepdims=True)
                at_row = jnp.sum(jnp.where(row == j, s, 0.0), axis=0, keepdims=True)
                m_row = jnp.sum(jnp.where(row == j, m, 0.0), axis=0, keepdims=True)
                pivot = jnp.sum(jnp.where(row == j, at_lane, 0.0), axis=0, keepdims=True)
                pivot = pivot[:, 0:1]
                times = jnp.where(row[:, 0:1] > j, at_lane / pivot, 0.0)
                s = s - times * at_row
                m = m - times * m_row
                m = jnp.where(row == j, m_row * lax.rsqrt(pivot), m)
                return s, m

            _, m = lax.fori_loop(0, n, eliminate, (a, eye))
            scratch[i] = m

    for i, by_lane in enumerate(scales):
        scratch[i] = scratch[i] * by_lane


def first_factor_kernel(col, far_ids, g0, m, mt, order):
    w, c = lax.axis_index("wide"), lax.axis_index("col")
    slots = far_ids.shape[1]

    def clear(p, carry):
        order[0, p] = slots
        return carry

    def put(s, carry):
        cluster = far_ids[0, s]

        @pl.when(cluster >= 0)
        def _():
            dc = lax.rem(cluster, col) - c + REACH
            dw = lax.div(cluster, col) - w + REACH
            order[0, dc * SPAN + dw] = s

        return carry

    lax.fori_loop(0, SPAN * SPAN, clear, 0)
    lax.fori_loop(0, slots, put, 0)
    inverse_factors([g0[...]], m)
    mt[...] = m[0].T


def second_factor_kernel(gram, m, mt, u):
    k = gram.shape[1]
    h = gram[0:k, :]
    n = gram[k:, :]
    inverse_factors([n - t_dot_full(h, h), n], m)
    mt[...] = m[0].T
    u[...] = -dot_full(h, mt[...])


def last_kernel(step, g0, m0, gram1, mn, gram2, z1, z2, out, m):
    k = g0.shape[1]
    down = ((0,), (0,))
    beta = dot_three(m0[0], g0[...])
    h1, h2 = gram1[0:k, :], gram2[0:k, :]
    n12, n22 = gram2[k : 2 * k, :], gram2[2 * k :, :]
    first = mn[1]
    b1 = dot_three(first, dot_three(h1, beta, down))
    t = dot_full(first, n12)
    inverse_factors([n22 - t_dot_full(t, t)], m)
    b2 = dot_three(h2, beta, down) - dot_three(t, b1, down)
    y2 = dot_three(m[0], dot_three(m[0], b2), down)
    y1 = dot_three(first, b1 - dot_three(t, y2), down)

    def combine(i, carry):
        piece = pl.ds(pl.multiple_of(i * step, step), step)
        out[piece, :] = dot_three(z1[piece, :], y1) + dot_three(z2[piece, :], y2)
        return carry

    lax.fori_loop(0, out.shape[0] // step, combine, 0)


def on_device(
    wide, col, rhs, basis, self_block, near_block, near_ids, couplings, far_ids, starts, schwarz_inverse
):
    rows, width = rhs.shape
    rank = basis.shape[1]
    order = schwarz_inverse.shape[1]
    margin = (order - rows) // 2
    step = rows // 3
    slots, links = near_ids.shape[1], far_ids.shape[1]
    vmem = pl.BlockSpec(memory_space=pltpu.VMEM)
    smem = pl.BlockSpec(memory_space=pltpu.SMEM)
    anywhere = pl.BlockSpec(memory_space=pl.ANY)

    def block(n):
        return jax.ShapeDtypeStruct((n, width), F32)

    square = jax.ShapeDtypeStruct((1, width, width), F32)
    local = pltpu.CompilerParams(vmem_limit_bytes=VMEM_BYTES)

    def talks(number):
        return pltpu.CompilerParams(
            collective_id=number, has_side_effects=True, vmem_limit_bytes=VMEM_BYTES
        )

    gram0 = pl.pallas_call(
        functools.partial(first_gram_kernel, wide, col, step),
        out_shape=block(width),
        in_specs=[vmem],
        out_specs=vmem,
        scratch_shapes=reduce_scratch(width, width, wide, col),
        compiler_params=talks(0),
        name="first_gram",
    )(rhs)
    m0, mt0, listed = pl.pallas_call(
        functools.partial(first_factor_kernel, col),
        out_shape=(square, block(width), jax.ShapeDtypeStruct((1, SPAN * SPAN), jnp.int32)),
        in_specs=[smem, vmem],
        out_specs=(vmem, vmem, smem),
        compiler_params=local,
        name="first_factor",
    )(far_ids, gram0)

    def take_step(first, *blocks):
        grams = 2 if first else 3
        outs = [block(rows)] * 3 if first else [block(rows)]
        held = [] if first else [pltpu.VMEM((rows, width), F32)] * 2
        dma = pltpu.SemaphoreType.DMA
        return pl.pallas_call(
            functools.partial(step_kernel, wide, col, step, first),
            out_shape=(*outs, block(grams * width)),
            in_specs=[smem] * 3 + [vmem] * len(blocks) + [anywhere] * 5,
            out_specs=(vmem,) * (len(outs) + 1),
            scratch_shapes=held
            + [
                pltpu.VMEM((rows, rank), BF16),
                pltpu.VMEM((rows, rows), BF16),
                pltpu.VMEM((slots, rows, rows), BF16),
                pltpu.VMEM((links + 1, rank, rank), BF16),
                pltpu.VMEM((order, order), BF16),
                pltpu.VMEM((2, margin, width), BF16),
                pltpu.VMEM((order, width), BF16),
                pltpu.VMEM((margin, width), F32),
                pltpu.VMEM((margin, width), F32),
                pltpu.VMEM((2, margin, width), F32),
                pltpu.VMEM((10, rows, width), BF16),
                pltpu.VMEM((SPAN * SPAN, rank, width), BF16),
                pltpu.VMEM((rank, width), F32),
                dma((5,)),
                dma((4,)),
                dma((4,)),
                dma((9,)),
                dma((9,)),
                dma((SPAN,)),
                dma((SPAN,)),
                dma((SPAN * (REACH + 1),)),
                dma((SPAN * (REACH + 1),)),
                dma((SPAN * (REACH + 1),)),
                dma((SPAN * REACH,)),
                dma((SPAN * REACH,)),
            ]
            + reduce_scratch(grams * width, width, wide, col),
            compiler_params=talks(1 if first else 2),
            name="first_step" if first else "second_step",
        )(starts, near_ids, listed, *blocks, basis, self_block, near_block, couplings, schwarz_inverse)

    v1, z1, w1, gram1 = take_step(True, rhs, mt0)
    m1, mt1, u = pl.pallas_call(
        second_factor_kernel,
        out_shape=(jax.ShapeDtypeStruct((2, width, width), F32), block(width), block(width)),
        in_specs=[vmem],
        out_specs=(vmem,) * 3,
        compiler_params=local,
        name="second_factor",
    )(gram1)
    z2, gram2 = take_step(False, w1, mt1, v1, u)
    return pl.pallas_call(
        functools.partial(last_kernel, step),
        out_shape=block(rows),
        in_specs=[vmem] * 7,
        out_specs=vmem,
        scratch_shapes=[pltpu.VMEM((1, width, width), F32)],
        compiler_params=local,
        name="last",
    )(gram0, m0, gram1, m1, gram2, z1, z2)


def solution(mesh):
    in_specs = (
        P(("wide", "col"), None),
        P(("wide", "col"), None),
        P(("wide", "col"), None),
        P(("wide", "col"), None, None, None),
        P(("wide", "col"), None),
        P(("wide", "col"), None, None, None),
        P(("wide", "col"), None),
        P(("wide", "col"), None),
        P(("wide", "col"), None, None),
    )
    out_specs = P(("wide", "col"), None)
    return jax.shard_map(
        functools.partial(on_device, mesh.shape["wide"], mesh.shape["col"]),
        mesh=mesh,
        in_specs=in_specs,
        out_specs=out_specs,
        check_vma=False,
    )
```

```python
import functools

import jax
import jax.numpy as jnp
from jax import lax
from jax.experimental import pallas as pl
from jax.experimental.pallas import tpu as pltpu
from jax.sharding import PartitionSpec as P

REACH = 3
SPAN = 2 * REACH + 1
MESH = pl.DeviceIdType.MESH
HIGHEST = lax.Precision.HIGHEST
F32 = jnp.float32
BF16 = jnp.bfloat16
VMEM_BYTES = 60 * 1024 * 1024


def dot(left, right):
    return jnp.dot(left, right, preferred_element_type=F32)


def dot_full(left, right):
    return jnp.dot(left, right, precision=HIGHEST, preferred_element_type=F32)


def dot_full_t(left, right):
    return lax.dot_general(
        left, right, (((1,), (1,)), ((), ())), precision=HIGHEST, preferred_element_type=F32
    )


def t_dot_full(left, right):
    return lax.dot_general(
        left, right, (((0,), (0,)), ((), ())), precision=HIGHEST, preferred_element_type=F32
    )


def two_parts(value):
    high = value.astype(BF16)
    return high, (value - high.astype(F32)).astype(BF16)


def dot_three(left, right, dims=((1,), (0,))):
    lh, ll = two_parts(left)
    rh, rl = two_parts(right)

    def one(a, b):
        return lax.dot_general(a, b, (dims, ((), ())), preferred_element_type=F32)

    return (one(lh, rl) + one(ll, rh)) + one(lh, rh)


def picks(start, count, total):
    row = lax.broadcasted_iota(jnp.int32, (count, total), 0)
    lane = lax.broadcasted_iota(jnp.int32, (count, total), 1)
    return jnp.where(lane - row == start, 1.0, 0.0).astype(BF16)


def places(start, count, total):
    row = lax.broadcasted_iota(jnp.int32, (total, count), 0)
    lane = lax.broadcasted_iota(jnp.int32, (total, count), 1)
    return jnp.where(row - lane == start, 1.0, 0.0).astype(BF16)


def three_parts(value):
    high = value.astype(BF16)
    rest = value - high.astype(F32)
    mid = rest.astype(BF16)
    return high, mid, (rest - mid.astype(F32)).astype(BF16)


def remote(src, dst, send_sem, recv_sem, w, c):
    return pltpu.make_async_remote_copy(
        src_ref=src,
        dst_ref=dst,
        send_sem=send_sem,
        recv_sem=recv_sem,
        device_id=(w, c),
        device_id_type=MESH,
    )


def greet(w, c, wide, col):
    barrier = pltpu.get_barrier_semaphore()

    def along_col(k, carry):
        pl.semaphore_signal(
            barrier, inc=1, device_id=(w, lax.rem(c + k, col)), device_id_type=MESH
        )
        return carry

    def along_wide(k, carry):
        pl.semaphore_signal(
            barrier, inc=1, device_id=(lax.rem(w + k, wide), c), device_id_type=MESH
        )
        return carry

    lax.fori_loop(1, col, along_col, 0)
    lax.fori_loop(1, wide, along_wide, 0)


def meet(wide, col):
    pl.semaphore_wait(pltpu.get_barrier_semaphore(), wide + col - 2)


def all_reduce(w, c, wide, col, g, half, land, ysl, out, send, recv):
    rows = g.shape[0]
    high = rows // 2
    part = high // col
    core = lax.rem(w, 2)
    y = w // 2
    ys = wide // 2
    partner = w + 1 - 2 * core
    mine = pl.multiple_of(core * high, high)
    other = pl.multiple_of((1 - core) * high, high)
    own = pl.multiple_of(mine + c * part, part)

    swap = remote(g.at[pl.ds(other, high)], half, send.at[0], recv.at[0], partner, c)
    swap.start()
    swap.wait()
    g[pl.ds(mine, high), :] += half[...]

    def scatter(k, carry):
        d = lax.rem(c + k, col)
        remote(
            g.at[pl.ds(pl.multiple_of(mine + d * part, part), part)],
            land.at[pl.ds(pl.multiple_of((col - 1 - k) * part, part), part)],
            send.at[1],
            recv.at[1],
            w,
            d,
        ).start()
        return carry

    lax.fori_loop(1, col, scatter, 0)
    many = (col - 1) * part
    remote(g.at[pl.ds(0, many)], land, send.at[1], recv.at[1], w, c).wait()
    total = g[pl.ds(own, part), :]
    for k in range(col - 1):
        total += land[k * part : (k + 1) * part, :]
    ysl[y] = total

    def spread(k, carry):
        other_y = lax.rem(y + k, ys)
        remote(ysl.at[y], ysl.at[y], send.at[2], recv.at[2], 2 * other_y + core, c).start()
        return carry

    lax.fori_loop(1, ys, spread, 0)
    few = pl.ds(0, ys - 1)
    remote(ysl.at[few], ysl.at[few], send.at[2], recv.at[2], w, c).wait()
    total = ysl[0]
    for k in range(1, ys):
        total += ysl[k]
    out[pl.ds(own, part), :] = total

    def gather(k, carry):
        d = lax.rem(c + k, col)
        spot = pl.ds(own, part)
        remote(out.at[spot], out.at[spot], send.at[3], recv.at[3], w, d).start()
        return carry

    lax.fori_loop(1, col, gather, 0)
    spot = pl.ds(0, many)
    remote(out.at[spot], out.at[spot], send.at[3], recv.at[3], w, c).wait()
    spot = pl.ds(mine, high)
    swap = remote(out.at[spot], out.at[spot], send.at[4], recv.at[4], partner, c)
    swap.start()
    swap.wait()


def reduce_scratch(rows, width, wide, col):
    high = rows // 2
    part = high // col
    return [
        pltpu.VMEM((rows, width), F32),
        pltpu.VMEM((high, width), F32),
        pltpu.VMEM(((col - 1) * part, width), F32),
        pltpu.VMEM((wide // 2, part, width), F32),
        pltpu.SemaphoreType.DMA((5,)),
        pltpu.SemaphoreType.DMA((5,)),
    ]


def local_grams(lefts, right, g, step):
    width = right.shape[1]
    rows = right.shape[0]
    for i, left in enumerate(lefts):
        spot = slice(i * width, (i + 1) * width)
        g[spot, :] = dot_three(left[0:step, :], right[0:step, :], ((0,), (0,)))

        def add(k, carry, left=left, spot=spot):
            piece = pl.ds(pl.multiple_of(k * step, step), step)
            g[spot, :] += dot_three(left[piece, :], right[piece, :], ((0,), (0,)))
            return carry

        lax.fori_loop(1, rows // step, add, 0)


def clear_ends(halo, c, col):
    for i, end in ((0, 0), (1, col - 1)):

        @pl.when(c == end)
        def _(i=i):
            halo[i] = jnp.zeros(halo.shape[1:], F32)


def pick_rows(starts, block, stage):
    margin, rows = stage.shape[1], block.shape[0]
    for i in range(2):
        chosen = picks(starts[0, 1 - i], margin, rows)
        high, mid, low = three_parts(block[...])
        stage[i] = (dot(chosen, low) + dot(chosen, mid)) + dot(chosen, high)


def halo_copies(stage, halo, send, recv, w, c, col):
    return (
        (c < col - 1, c > 0, remote(stage.at[0], halo.at[0], send.at[0], recv.at[0], w, c + 1)),
        (c > 0, c < col - 1, remote(stage.at[1], halo.at[1], send.at[1], recv.at[1], w, c - 1)),
    )


def first_gram_kernel(
    wide, col, step, starts, rhs, out, halo, stage, hs, hr, g, half, land, ysl, send, recv
):
    w, c = lax.axis_index("wide"), lax.axis_index("col")
    clear_ends(halo, c, col)
    greet(w, c, wide, col)
    local_grams([rhs], rhs, g, step)
    pick_rows(starts, rhs, stage)
    meet(wide, col)
    copies = halo_copies(stage, halo, hs, hr, w, c, col)
    for sends, _, copy in copies:
        pl.when(sends)(copy.start)
    all_reduce(w, c, wide, col, g, half, land, ysl, out, send, recv)
    for sends, takes, copy in copies:
        pl.when(sends)(copy.wait_send)
        pl.when(takes)(copy.wait_recv)


def step_kernel(wide, col, step, first, *refs):
    if first:
        (starts, near_ids, order, x, mt, halo_x, basis_h, self_h, near_h, coup_h, sch_h, *rest) = refs
        (v, z, wv, halo_v, halo_w, gram, *rest) = rest
    else:
        (starts, near_ids, order, x, mt, halo_x, vprev, u, halo_vprev, basis_h, self_h, near_h, coup_h, sch_h, *rest) = refs
        (z, gram, v, wv, *rest) = rest
    (basis, selfb, near, coup, sch, stage, dom, pad_next, pad_prev, edge, nb, win, far, *rest) = rest
    (load, hs, hr, ns, nr, ws, wr, rs, rr, es, ps, pr, *reduce) = rest
    g, half, land, ysl, send, recv = reduce
    w, c = lax.axis_index("wide"), lax.axis_index("col")
    core = lax.rem(w, 2)
    partner = w + 1 - 2 * core
    rows, width = x.shape
    margin = edge.shape[1]
    has_prev, has_next = c > 0, c < col - 1

    loads = [
        pltpu.make_async_copy(sch_h.at[0], sch, load.at[0]),
        pltpu.make_async_copy(basis_h, basis, load.at[1]),
        pltpu.make_async_copy(self_h, selfb, load.at[2]),
        pltpu.make_async_copy(near_h.at[0], near, load.at[3]),
        pltpu.make_async_copy(
            coup_h.at[0], coup.at[pl.ds(0, coup_h.shape[1])], load.at[4]
        ),
    ]
    for copy in loads:
        copy.start()

    @pl.when(jnp.logical_not(has_prev))
    def _():
        pad_prev[...] = jnp.zeros((margin, width), F32)

    @pl.when(jnp.logical_not(has_next))
    def _():
        pad_next[...] = jnp.zeros((margin, width), F32)

    for i in range(SPAN):
        for a in range(SPAN):
            dc, dw = i - REACH, a - REACH
            off = (w + dw < 0) | (w + dw >= wide) | (c + dc < 0) | (c + dc >= col)
            if (dw or dc) and max(abs(dw), abs(dc)) > 1:

                @pl.when(off)
                def _(cell=i * SPAN + a):
                    win[cell] = jnp.zeros(win.shape[1:], BF16)

    if first:
        clear_ends(halo_w, c, col)
    greet(w, c, wide, col)

    def make_v(k, carry):
        piece = pl.ds(pl.multiple_of(k * step, step), step)
        value = dot_full(x[piece, :], mt[...])
        if not first:
            value += dot_full(vprev[piece, :], u[...])
        v[piece, :] = value
        dom[pl.ds(pl.multiple_of(margin + k * step, step), step), :] = value.astype(BF16)
        return carry

    lax.fori_loop(0, rows // step, make_v, 0)
    start_prev, start_next = starts[0, 0], starts[0, 1]
    for i, place in ((0, 0), (1, margin + rows)):
        value = dot_full(halo_x[i], mt[...])
        if first:
            halo_v[i] = value
        else:
            value += dot_full(halo_vprev[i], u[...])
        dom[place : place + margin, :] = value.astype(BF16)

    out_prev = remote(
        edge.at[0], pad_next, hs.at[2], hr.at[2], w, c - 1
    )
    out_next = remote(
        edge.at[1], pad_prev, hs.at[3], hr.at[3], w, c + 1
    )
    nb[9] = jnp.zeros((rows, width), BF16)

    loads[0].wait()
    edge[0] = dot(sch[0:margin, :], dom[...])
    meet(wide, col)
    pl.when(has_prev)(out_prev.start)
    edge[1] = dot(sch[margin + rows :, :], dom[...])
    pl.when(has_next)(out_next.start)

    def solve(k, carry):
        piece = pl.ds(pl.multiple_of(k * step, step), step)
        z[piece, :] = dot(sch[pl.ds(pl.multiple_of(margin + k * step, step), step), :], dom[...])
        return carry

    lax.fori_loop(0, rows // step, solve, 0)
    pl.when(has_next)(out_prev.wait_recv)
    pl.when(has_prev)(out_next.wait_recv)
    for start, pad in ((start_next, pad_next), (start_prev, pad_prev)):
        spread = places(start, margin, rows)
        for part in three_parts(pad[...]):
            z[...] += dot(spread, part)
    nb[4] = z[...].astype(BF16)
    loads[1].wait()

    def near_to(dw, dc, source):
        return remote(
            nb.at[source], nb.at[(1 - dw) * 3 + dc + 1], ns.at[(1 - dw) * 3 + dc + 1],
            nr.at[(1 - dw) * 3 + dc + 1], w + dw, c,
        )

    def near_col(dc):
        return remote(nb.at[4], nb.at[4 - dc], ns.at[4 - dc], nr.at[4 - dc], w, c + dc)

    beside = {-1: has_prev, 1: has_next}
    within = {d: (w + d >= 0) & (w + d < wide) for d in range(-REACH, REACH + 1) if d}
    for d in (-1, 1):
        pl.when(beside[d])(near_col(d).start)
    centre = REACH * SPAN + REACH
    win[centre] = lax.dot_general(
        basis[...], nb[4], (((0,), (0,)), ((), ())), preferred_element_type=F32
    ).astype(BF16)

    def far_wide(d):
        return remote(
            win.at[centre], win.at[centre - d], ws.at[REACH - d], wr.at[REACH - d], w + d, c
        )

    for d in (1, -1, 2, -2, 3, -3):
        pl.when(within[d])(far_wide(d).start)
    for d in (-1, 1):
        pl.when(within[d])(near_to(d, 0, 4).start)

    def on_grid(a):
        return (w + a - REACH >= 0) & (w + a - REACH < wide)

    def hand_on(direction, k, j):
        held = REACH - direction * (k - 1)
        lands = held - direction
        a = REACH * core + j
        return remote(
            win.at[held * SPAN + a], win.at[lands * SPAN + a],
            rs.at[lands * (REACH + 1) + j], rr.at[lands * (REACH + 1) + j], w, c + direction,
        )

    def jump(direction, j):
        lands = REACH - direction * REACH
        a = REACH * core + j
        return remote(
            win.at[(REACH + direction) * SPAN + a], win.at[lands * SPAN + a],
            rs.at[lands * (REACH + 1) + j], rr.at[lands * (REACH + 1) + j],
            w, c + direction * (REACH + 1),
        )

    def jumps(direction):
        return c + REACH + 1 < col if direction > 0 else c - REACH - 1 >= 0

    def from_end(direction, j):
        lands = REACH - direction * REACH
        a = REACH * core + j
        return remote(
            win.at[REACH * SPAN + a], win.at[lands * SPAN + a],
            es.at[lands * (REACH + 1) + j], rr.at[lands * (REACH + 1) + j],
            w, c + direction * REACH,
        )

    def at_end(direction):
        if direction > 0:
            return (c == 0) & (c + REACH < col)
        return (c == col - 1) & (c - REACH >= 0)

    def share(i, j):
        return remote(
            win.at[i * SPAN + 1 + 2 * core + j], win.at[i * SPAN + (REACH + 1) * core + j],
            ps.at[i * REACH + j], pr.at[i * REACH + j], partner, c,
        )

    def arrives(direction, k):
        return c - k >= 0 if direction > 0 else c + k < col

    def sends(direction, k):
        held = c - (k - 1) >= 0 if direction > 0 else c + (k - 1) < col
        return held & beside[direction]

    def each(count, body):
        def run(j, carry):
            body(j)
            return carry

        lax.fori_loop(0, count, run, 0)

    def pass_on(direction, k):
        def row(j):
            here = arrives(direction, k) & on_grid(REACH * core + j)

            @pl.when(here)
            def _():
                hand_on(direction, k, j).wait_recv()

            if k == 1:
                @pl.when(here & jumps(-direction))
                def _():
                    jump(-direction, j).start()

            if k + 1 < REACH:
                @pl.when(sends(direction, k + 1) & on_grid(REACH * core + j))
                def _():
                    hand_on(direction, k + 1, j).start()

        each(REACH + 1, row)
        i = REACH - direction * k

        def across(j):
            @pl.when(arrives(direction, k) & on_grid(1 + 2 * core + j))
            def _():
                share(i, j).start()

        each(REACH, across)

    def take_share(direction, k):
        i = REACH - direction * k

        def row(j):
            @pl.when(arrives(direction, k) & on_grid((REACH + 1) * (1 - core) + j))
            def _():
                share(i, j).wait_recv()

        each(REACH, row)

    def far_strip(i):
        total = None
        for a in range(SPAN):
            if abs(i - REACH) > 1 or abs(a - REACH) > 1:
                term = dot(coup[order[0, i * SPAN + a]], win[i * SPAN + a])
                total = term if total is None else total + term
        far[...] += total

    for d in within:
        pl.when(within[-d])(far_wide(d).wait_recv)

    def first_hand(j):
        for d in (1, -1):
            @pl.when(beside[d] & on_grid(REACH * core + j))
            def _(d=d):
                hand_on(d, 1, j).start()

            @pl.when(at_end(d) & on_grid(REACH * core + j))
            def _(d=d):
                from_end(d, j).start()

    each(REACH + 1, first_hand)

    loads[2].wait()
    wv[...] = dot(selfb[...], nb[4])

    for d in (-1, 1):
        pl.when(beside[d])(near_col(-d).wait_recv)
        for e in (-1, 1):
            pl.when(beside[d] & within[e])(near_to(e, d, 4 + d).start)

    loads[4].wait()
    coup[coup.shape[0] - 1] = jnp.zeros(coup.shape[1:], BF16)
    far[...] = jnp.zeros_like(far)
    far_strip(REACH)
    for d in (1, -1):
        pass_on(d, 1)
    for d in (1, -1):
        take_share(d, 1)
    far_strip(REACH - 1)
    far_strip(REACH + 1)
    for e in (-1, 1):
        for d in (-1, 0, 1):
            ok = within[-e] if d == 0 else within[-e] & beside[d]
            pl.when(ok)(near_to(e, d, 4 + d).wait_recv)
    loads[3].wait()

    def near_slot(s, carry):
        cluster = near_ids[0, s]
        place = (lax.div(cluster, col) - w + 1) * 3 + (lax.rem(cluster, col) - c + 1)
        place = jnp.where(cluster >= 0, jnp.minimum(jnp.maximum(place, 0), 8), 9)
        wv[...] += dot(near[s], nb[place])
        return carry

    lax.fori_loop(0, near_ids.shape[1], near_slot, 0)
    for d in (1, -1):
        pass_on(d, 2)
        pass_on(d, 3)
    for d in (1, -1):
        take_share(d, 2)
    far_strip(REACH - 2)
    far_strip(REACH + 2)
    for d in (1, -1):
        take_share(d, 3)
    far_strip(REACH - 3)
    far_strip(REACH + 3)
    wv[...] += dot(basis[...], far[...].astype(BF16))
    if first:
        pick_rows(starts, wv, stage)
        copies = halo_copies(stage, halo_w, hs, hr, w, c, col)
        for goes, _, copy in copies:
            pl.when(goes)(copy.start)
    local_grams([v, wv] if first else [vprev, x, wv], wv, g, step)

    pl.when(has_prev)(out_prev.wait_send)
    pl.when(has_next)(out_next.wait_send)
    for d in (-1, 1):
        pl.when(beside[d])(near_col(d).wait_send)
        pl.when(within[d])(near_to(d, 0, 4).wait_send)
        for e in (-1, 1):
            pl.when(beside[d] & within[e])(near_to(e, d, 4 + d).wait_send)
    for d in within:
        pl.when(within[d])(far_wide(d).wait_send)
    for k in range(1, REACH + 1):
        for d in (1, -1):

            def sent(j, d=d, k=k):
                if k < REACH:
                    @pl.when(sends(d, k) & on_grid(REACH * core + j))
                    def _():
                        hand_on(d, k, j).wait_send()
                else:
                    @pl.when(arrives(-d, 1) & jumps(d) & on_grid(REACH * core + j))
                    def _():
                        jump(d, j).wait_send()

                    @pl.when(at_end(d) & on_grid(REACH * core + j))
                    def _():
                        from_end(d, j).wait_send()

            def shared(j, d=d, k=k):
                @pl.when(arrives(d, k) & on_grid(1 + 2 * core + j))
                def _():
                    share(REACH - d * k, j).wait_send()

            each(REACH + 1, sent)
            each(REACH, shared)

    all_reduce(w, c, wide, col, g, half, land, ysl, gram, send, recv)
    if first:
        for goes, takes, copy in copies:
            pl.when(goes)(copy.wait_send)
            pl.when(takes)(copy.wait_recv)


def inverse_factors(matrices, scratch):
    n = matrices[0].shape[0]
    row = lax.broadcasted_iota(jnp.int32, (n, n), 0)
    lane = lax.broadcasted_iota(jnp.int32, (n, n), 1)
    eye = (row == lane).astype(F32)

    def lower(e):
        return jnp.where(row > lane, e, 0.5 * e * eye)

    scaled, scales = [], []
    for i, a in enumerate(matrices):
        only = a * eye
        by_row = lax.rsqrt(jnp.sum(only, axis=1, keepdims=True))
        by_lane = lax.rsqrt(jnp.sum(only, axis=0, keepdims=True))
        a = a * by_row * by_lane
        scratch[i] = eye - lower(a - eye)
        scaled.append(a)
        scales.append(by_lane)
    limit = 1e-5

    def go_on(state):
        step, error = state
        return (step < 8) & jnp.logical_not(error < limit)

    def refine(state):
        step, _ = state
        error = jnp.float32(0.0)
        for i, a in enumerate(scaled):
            m = scratch[i]
            e = dot_full_t(dot_full(m, a), m) - eye
            scratch[i] = m - dot_three(lower(e), m)
            error = error + jnp.sum(e * e)
        return step + 1, error

    _, error = lax.while_loop(go_on, refine, (jnp.int32(0), jnp.float32(1.0)))

    @pl.when(jnp.logical_not(error < limit))
    def _():
        for i, a in enumerate(scaled):

            def eliminate(j, state):
                s, m = state
                at_lane = jnp.sum(jnp.where(lane == j, s, 0.0), axis=1, keepdims=True)
                at_row = jnp.sum(jnp.where(row == j, s, 0.0), axis=0, keepdims=True)
                m_row = jnp.sum(jnp.where(row == j, m, 0.0), axis=0, keepdims=True)
                pivot = jnp.sum(jnp.where(row == j, at_lane, 0.0), axis=0, keepdims=True)
                pivot = pivot[:, 0:1]
                times = jnp.where(row[:, 0:1] > j, at_lane / pivot, 0.0)
                s = s - times * at_row
                m = m - times * m_row
                m = jnp.where(row == j, m_row * lax.rsqrt(pivot), m)
                return s, m

            _, m = lax.fori_loop(0, n, eliminate, (a, eye))
            scratch[i] = m

    for i, by_lane in enumerate(scales):
        scratch[i] = scratch[i] * by_lane


def first_factor_kernel(col, far_ids, g0, m, mt, order):
    w, c = lax.axis_index("wide"), lax.axis_index("col")
    slots = far_ids.shape[1]

    def clear(p, carry):
        order[0, p] = slots
        return carry

    def put(s, carry):
        cluster = far_ids[0, s]

        @pl.when(cluster >= 0)
        def _():
            dc = lax.rem(cluster, col) - c + REACH
            dw = lax.div(cluster, col) - w + REACH
            order[0, dc * SPAN + dw] = s

        return carry

    lax.fori_loop(0, SPAN * SPAN, clear, 0)
    lax.fori_loop(0, slots, put, 0)
    inverse_factors([g0[...]], m)
    mt[...] = m[0].T


def second_factor_kernel(gram, m, mt, u):
    k = gram.shape[1]
    h = gram[0:k, :]
    n = gram[k:, :]
    inverse_factors([n - t_dot_full(h, h), n], m)
    mt[...] = m[0].T
    u[...] = -dot_full(h, mt[...])


def last_kernel(step, g0, m0, gram1, mn, gram2, z1, z2, out, m):
    k = g0.shape[1]
    down = ((0,), (0,))
    beta = dot_three(m0[0], g0[...])
    h1, h2 = gram1[0:k, :], gram2[0:k, :]
    n12, n22 = gram2[k : 2 * k, :], gram2[2 * k :, :]
    first = mn[1]
    b1 = dot_three(first, dot_three(h1, beta, down))
    t = dot_full(first, n12)
    inverse_factors([n22 - t_dot_full(t, t)], m)
    b2 = dot_three(h2, beta, down) - dot_three(t, b1, down)
    y2 = dot_three(m[0], dot_three(m[0], b2), down)
    y1 = dot_three(first, b1 - dot_three(t, y2), down)

    def combine(i, carry):
        piece = pl.ds(pl.multiple_of(i * step, step), step)
        out[piece, :] = dot_three(z1[piece, :], y1) + dot_three(z2[piece, :], y2)
        return carry

    lax.fori_loop(0, out.shape[0] // step, combine, 0)


def on_device(
    wide, col, rhs, basis, self_block, near_block, near_ids, couplings, far_ids, starts, schwarz_inverse
):
    rows, width = rhs.shape
    rank = basis.shape[1]
    order = schwarz_inverse.shape[1]
    margin = (order - rows) // 2
    step = rows // 3
    slots, links = near_ids.shape[1], far_ids.shape[1]
    vmem = pl.BlockSpec(memory_space=pltpu.VMEM)
    smem = pl.BlockSpec(memory_space=pltpu.SMEM)
    anywhere = pl.BlockSpec(memory_space=pl.ANY)

    def block(n):
        return jax.ShapeDtypeStruct((n, width), F32)

    square = jax.ShapeDtypeStruct((1, width, width), F32)
    local = pltpu.CompilerParams(vmem_limit_bytes=VMEM_BYTES)

    def talks(number):
        return pltpu.CompilerParams(
            collective_id=number, has_side_effects=True, vmem_limit_bytes=VMEM_BYTES
        )

    halo = jax.ShapeDtypeStruct((2, margin, width), F32)
    gram0, halo_x = pl.pallas_call(
        functools.partial(first_gram_kernel, wide, col, step),
        out_shape=(block(width), halo),
        in_specs=[smem, vmem],
        out_specs=(vmem, vmem),
        scratch_shapes=[
            pltpu.VMEM((2, margin, width), F32),
            pltpu.SemaphoreType.DMA((2,)),
            pltpu.SemaphoreType.DMA((2,)),
        ]
        + reduce_scratch(width, width, wide, col),
        compiler_params=talks(0),
        name="first_gram",
    )(starts, rhs)
    m0, mt0, listed = pl.pallas_call(
        functools.partial(first_factor_kernel, col),
        out_shape=(square, block(width), jax.ShapeDtypeStruct((1, SPAN * SPAN), jnp.int32)),
        in_specs=[smem, vmem],
        out_specs=(vmem, vmem, smem),
        compiler_params=local,
        name="first_factor",
    )(far_ids, gram0)

    def take_step(first, *blocks):
        grams = 2 if first else 3
        outs = [block(rows)] * 3 + [halo] * 2 if first else [block(rows)]
        held = [] if first else [pltpu.VMEM((rows, width), F32)] * 2
        dma = pltpu.SemaphoreType.DMA
        return pl.pallas_call(
            functools.partial(step_kernel, wide, col, step, first),
            out_shape=(*outs, block(grams * width)),
            in_specs=[smem] * 3 + [vmem] * len(blocks) + [anywhere] * 5,
            out_specs=(vmem,) * (len(outs) + 1),
            scratch_shapes=held
            + [
                pltpu.VMEM((rows, rank), BF16),
                pltpu.VMEM((rows, rows), BF16),
                pltpu.VMEM((slots, rows, rows), BF16),
                pltpu.VMEM((links + 1, rank, rank), BF16),
                pltpu.VMEM((order, order), BF16),
                pltpu.VMEM((2, margin, width), F32),
                pltpu.VMEM((order, width), BF16),
                pltpu.VMEM((margin, width), F32),
                pltpu.VMEM((margin, width), F32),
                pltpu.VMEM((2, margin, width), F32),
                pltpu.VMEM((10, rows, width), BF16),
                pltpu.VMEM((SPAN * SPAN, rank, width), BF16),
                pltpu.VMEM((rank, width), F32),
                dma((5,)),
                dma((4,)),
                dma((4,)),
                dma((9,)),
                dma((9,)),
                dma((SPAN,)),
                dma((SPAN,)),
                dma((SPAN * (REACH + 1),)),
                dma((SPAN * (REACH + 1),)),
                dma((SPAN * (REACH + 1),)),
                dma((SPAN * REACH,)),
                dma((SPAN * REACH,)),
            ]
            + reduce_scratch(grams * width, width, wide, col),
            compiler_params=talks(1 if first else 2),
            name="first_step" if first else "second_step",
        )(starts, near_ids, listed, *blocks, basis, self_block, near_block, couplings, schwarz_inverse)

    v1, z1, w1, halo_v, halo_w, gram1 = take_step(True, rhs, mt0, halo_x)
    m1, mt1, u = pl.pallas_call(
        second_factor_kernel,
        out_shape=(jax.ShapeDtypeStruct((2, width, width), F32), block(width), block(width)),
        in_specs=[vmem],
        out_specs=(vmem,) * 3,
        compiler_params=local,
        name="second_factor",
    )(gram1)
    z2, gram2 = take_step(False, w1, mt1, halo_w, v1, u, halo_v)
    return pl.pallas_call(
        functools.partial(last_kernel, step),
        out_shape=block(rows),
        in_specs=[vmem] * 7,
        out_specs=vmem,
        scratch_shapes=[pltpu.VMEM((1, width, width), F32)],
        compiler_params=local,
        name="last",
    )(gram0, m0, gram1, m1, gram2, z1, z2)


def solution(mesh):
    in_specs = (
        P(("wide", "col"), None),
        P(("wide", "col"), None),
        P(("wide", "col"), None),
        P(("wide", "col"), None, None, None),
        P(("wide", "col"), None),
        P(("wide", "col"), None, None, None),
        P(("wide", "col"), None),
        P(("wide", "col"), None),
        P(("wide", "col"), None, None),
    )
    out_specs = P(("wide", "col"), None)
    return jax.shard_map(
        functools.partial(on_device, mesh.shape["wide"], mesh.shape["col"]),
        mesh=mesh,
        in_specs=in_specs,
        out_specs=out_specs,
        check_vma=False,
    )
```

```python
import functools

import jax
import jax.numpy as jnp
from jax import lax
from jax.experimental import pallas as pl
from jax.experimental.pallas import tpu as pltpu
from jax.sharding import PartitionSpec as P

REACH = 3
SPAN = 2 * REACH + 1
MESH = pl.DeviceIdType.MESH
HIGHEST = lax.Precision.HIGHEST
F32 = jnp.float32
BF16 = jnp.bfloat16
VMEM_BYTES = 60 * 1024 * 1024


def dot(left, right):
    return jnp.dot(left, right, preferred_element_type=F32)


def dot_full(left, right):
    return jnp.dot(left, right, precision=HIGHEST, preferred_element_type=F32)


def dot_full_t(left, right):
    return lax.dot_general(
        left, right, (((1,), (1,)), ((), ())), precision=HIGHEST, preferred_element_type=F32
    )


def t_dot_full(left, right):
    return lax.dot_general(
        left, right, (((0,), (0,)), ((), ())), precision=HIGHEST, preferred_element_type=F32
    )


def two_parts(value):
    high = value.astype(BF16)
    return high, (value - high.astype(F32)).astype(BF16)


def dot_three(left, right, dims=((1,), (0,))):
    lh, ll = two_parts(left)
    rh, rl = two_parts(right)

    def one(a, b):
        return lax.dot_general(a, b, (dims, ((), ())), preferred_element_type=F32)

    return (one(lh, rl) + one(ll, rh)) + one(lh, rh)


def picks(start, count, total):
    row = lax.broadcasted_iota(jnp.int32, (count, total), 0)
    lane = lax.broadcasted_iota(jnp.int32, (count, total), 1)
    return jnp.where(lane - row == start, 1.0, 0.0).astype(BF16)


def places(start, count, total):
    row = lax.broadcasted_iota(jnp.int32, (total, count), 0)
    lane = lax.broadcasted_iota(jnp.int32, (total, count), 1)
    return jnp.where(row - lane == start, 1.0, 0.0).astype(BF16)


def three_parts(value):
    high = value.astype(BF16)
    rest = value - high.astype(F32)
    mid = rest.astype(BF16)
    return high, mid, (rest - mid.astype(F32)).astype(BF16)


def remote(src, dst, send_sem, recv_sem, w, c):
    return pltpu.make_async_remote_copy(
        src_ref=src,
        dst_ref=dst,
        send_sem=send_sem,
        recv_sem=recv_sem,
        device_id=(w, c),
        device_id_type=MESH,
    )


def greet(w, c, wide, col):
    barrier = pltpu.get_barrier_semaphore()

    def along_col(k, carry):
        pl.semaphore_signal(
            barrier, inc=1, device_id=(w, lax.rem(c + k, col)), device_id_type=MESH
        )
        return carry

    def along_wide(k, carry):
        pl.semaphore_signal(
            barrier, inc=1, device_id=(lax.rem(w + k, wide), c), device_id_type=MESH
        )
        return carry

    lax.fori_loop(1, col, along_col, 0)
    lax.fori_loop(1, wide, along_wide, 0)


def meet(wide, col):
    pl.semaphore_wait(pltpu.get_barrier_semaphore(), wide + col - 2)


def all_reduce(w, c, wide, col, g, half, land, ysl, out, send, recv, others=()):
    rows = g.shape[0]
    high = rows // 2
    part = high // col
    core = lax.rem(w, 2)
    y = w // 2
    ys = wide // 2
    partner = w + 1 - 2 * core
    mine = pl.multiple_of(core * high, high)
    other = pl.multiple_of((1 - core) * high, high)
    own = pl.multiple_of(mine + c * part, part)

    swap = remote(g.at[pl.ds(other, high)], half, send.at[0], recv.at[0], partner, c)
    swap.start()
    swap.wait()
    g[pl.ds(mine, high), :] += half[...]

    def scatter(k, carry):
        d = lax.rem(c + k, col)
        remote(
            g.at[pl.ds(pl.multiple_of(mine + d * part, part), part)],
            land.at[pl.ds(pl.multiple_of((col - 1 - k) * part, part), part)],
            send.at[1],
            recv.at[1],
            w,
            d,
        ).start()
        return carry

    lax.fori_loop(1, col, scatter, 0)
    for goes, _, copy in others:
        pl.when(goes)(copy.start)
    many = (col - 1) * part
    remote(g.at[pl.ds(0, many)], land, send.at[1], recv.at[1], w, c).wait()
    total = g[pl.ds(own, part), :]
    for k in range(col - 1):
        total += land[k * part : (k + 1) * part, :]
    ysl[y] = total

    def spread(k, carry):
        other_y = lax.rem(y + k, ys)
        remote(ysl.at[y], ysl.at[y], send.at[2], recv.at[2], 2 * other_y + core, c).start()
        return carry

    lax.fori_loop(1, ys, spread, 0)
    few = pl.ds(0, ys - 1)
    remote(ysl.at[few], ysl.at[few], send.at[2], recv.at[2], w, c).wait()
    total = ysl[0]
    for k in range(1, ys):
        total += ysl[k]
    out[pl.ds(own, part), :] = total

    def gather(k, carry):
        d = lax.rem(c + k, col)
        spot = pl.ds(own, part)
        remote(out.at[spot], out.at[spot], send.at[3], recv.at[3], w, d).start()
        return carry

    lax.fori_loop(1, col, gather, 0)
    spot = pl.ds(0, many)
    remote(out.at[spot], out.at[spot], send.at[3], recv.at[3], w, c).wait()
    spot = pl.ds(mine, high)
    swap = remote(out.at[spot], out.at[spot], send.at[4], recv.at[4], partner, c)
    swap.start()
    swap.wait()
    for goes, takes, copy in others:
        pl.when(goes)(copy.wait_send)
        pl.when(takes)(copy.wait_recv)


def reduce_scratch(rows, width, wide, col):
    high = rows // 2
    part = high // col
    return [
        pltpu.VMEM((rows, width), F32),
        pltpu.VMEM((high, width), F32),
        pltpu.VMEM(((col - 1) * part, width), F32),
        pltpu.VMEM((wide // 2, part, width), F32),
        pltpu.SemaphoreType.DMA((5,)),
        pltpu.SemaphoreType.DMA((5,)),
    ]


def local_grams(lefts, right, g):
    width = right.shape[1]
    for i, left in enumerate(lefts):
        g[i * width : (i + 1) * width, :] = dot_three(left[...], right[...], ((0,), (0,)))


def clear_ends(halo, c, col):
    for i, end in ((0, 0), (1, col - 1)):

        @pl.when(c == end)
        def _(i=i):
            halo[i] = jnp.zeros(halo.shape[1:], F32)


def pick_rows(starts, block, stage):
    margin, rows = stage.shape[1], block.shape[0]
    for i in range(2):
        chosen = picks(starts[0, 1 - i], margin, rows)
        high, mid, low = three_parts(block[...])
        stage[i] = (dot(chosen, low) + dot(chosen, mid)) + dot(chosen, high)


def halo_copies(stage, halo, send, recv, w, c, col):
    return (
        (c < col - 1, c > 0, remote(stage.at[0], halo.at[0], send.at[0], recv.at[0], w, c + 1)),
        (c > 0, c < col - 1, remote(stage.at[1], halo.at[1], send.at[1], recv.at[1], w, c - 1)),
    )


def first_gram_kernel(
    wide, col, step, starts, rhs, out, halo, stage, hs, hr, g, half, land, ysl, send, recv
):
    w, c = lax.axis_index("wide"), lax.axis_index("col")
    clear_ends(halo, c, col)
    greet(w, c, wide, col)
    local_grams([rhs], rhs, g)
    pick_rows(starts, rhs, stage)
    meet(wide, col)
    copies = halo_copies(stage, halo, hs, hr, w, c, col)
    all_reduce(w, c, wide, col, g, half, land, ysl, out, send, recv, copies)


def step_kernel(wide, col, step, first, *refs):
    if first:
        (starts, near_ids, order, x, mt, halo_x, basis_h, self_h, near_h, coup_h, sch_h, *rest) = refs
        (v, z, wv, halo_v, halo_w, gram, *rest) = rest
    else:
        (starts, near_ids, order, x, mt, halo_x, vprev, u, halo_vprev, basis_h, self_h, near_h, coup_h, sch_h, *rest) = refs
        (z, gram, v, wv, *rest) = rest
    (basis, selfb, near, coup, sch, stage, dom, pad_next, pad_prev, edge, nb, win, far, *rest) = rest
    (load, hs, hr, ns, nr, ws, wr, rs, rr, es, ps, pr, *reduce) = rest
    g, half, land, ysl, send, recv = reduce
    w, c = lax.axis_index("wide"), lax.axis_index("col")
    core = lax.rem(w, 2)
    partner = w + 1 - 2 * core
    rows, width = x.shape
    margin = edge.shape[1]
    has_prev, has_next = c > 0, c < col - 1

    loads = [
        pltpu.make_async_copy(sch_h.at[0], sch, load.at[0]),
        pltpu.make_async_copy(basis_h, basis, load.at[1]),
        pltpu.make_async_copy(self_h, selfb, load.at[2]),
        pltpu.make_async_copy(near_h.at[0], near, load.at[3]),
        pltpu.make_async_copy(
            coup_h.at[0], coup.at[pl.ds(0, coup_h.shape[1])], load.at[4]
        ),
    ]
    for copy in loads:
        copy.start()

    @pl.when(jnp.logical_not(has_prev))
    def _():
        pad_prev[...] = jnp.zeros((margin, width), F32)

    @pl.when(jnp.logical_not(has_next))
    def _():
        pad_next[...] = jnp.zeros((margin, width), F32)

    for i in range(SPAN):
        for a in range(SPAN):
            dc, dw = i - REACH, a - REACH
            off = (w + dw < 0) | (w + dw >= wide) | (c + dc < 0) | (c + dc >= col)
            if (dw or dc) and max(abs(dw), abs(dc)) > 1:

                @pl.when(off)
                def _(cell=i * SPAN + a):
                    win[cell] = jnp.zeros(win.shape[1:], BF16)

    if first:
        clear_ends(halo_w, c, col)
    greet(w, c, wide, col)

    def make_v(k, carry):
        piece = pl.ds(pl.multiple_of(k * step, step), step)
        value = dot_full(x[piece, :], mt[...])
        if not first:
            value += dot_full(vprev[piece, :], u[...])
        v[piece, :] = value
        dom[pl.ds(pl.multiple_of(margin + k * step, step), step), :] = value.astype(BF16)
        return carry

    lax.fori_loop(0, rows // step, make_v, 0)
    start_prev, start_next = starts[0, 0], starts[0, 1]
    for i, place in ((0, 0), (1, margin + rows)):
        value = dot_full(halo_x[i], mt[...])
        if first:
            halo_v[i] = value
        else:
            value += dot_full(halo_vprev[i], u[...])
        dom[place : place + margin, :] = value.astype(BF16)

    out_prev = remote(
        edge.at[0], pad_next, hs.at[2], hr.at[2], w, c - 1
    )
    out_next = remote(
        edge.at[1], pad_prev, hs.at[3], hr.at[3], w, c + 1
    )
    nb[9] = jnp.zeros((rows, width), BF16)

    loads[0].wait()
    edge[0] = dot(sch[0:margin, :], dom[...])
    meet(wide, col)
    pl.when(has_prev)(out_prev.start)
    edge[1] = dot(sch[margin + rows :, :], dom[...])
    pl.when(has_next)(out_next.start)

    def solve(k, carry):
        piece = pl.ds(pl.multiple_of(k * step, step), step)
        z[piece, :] = dot(sch[pl.ds(pl.multiple_of(margin + k * step, step), step), :], dom[...])
        return carry

    lax.fori_loop(0, rows // step, solve, 0)
    pl.when(has_next)(out_prev.wait_recv)
    pl.when(has_prev)(out_next.wait_recv)
    for start, pad in ((start_next, pad_next), (start_prev, pad_prev)):
        spread = places(start, margin, rows)
        for part in three_parts(pad[...]):
            z[...] += dot(spread, part)
    nb[4] = z[...].astype(BF16)
    loads[1].wait()

    def near_to(dw, dc, source):
        return remote(
            nb.at[source], nb.at[(1 - dw) * 3 + dc + 1], ns.at[(1 - dw) * 3 + dc + 1],
            nr.at[(1 - dw) * 3 + dc + 1], w + dw, c,
        )

    def near_col(dc):
        return remote(nb.at[4], nb.at[4 - dc], ns.at[4 - dc], nr.at[4 - dc], w, c + dc)

    beside = {-1: has_prev, 1: has_next}
    within = {d: (w + d >= 0) & (w + d < wide) for d in range(-REACH, REACH + 1) if d}
    for d in (-1, 1):
        pl.when(beside[d])(near_col(d).start)
    centre = REACH * SPAN + REACH
    win[centre] = lax.dot_general(
        basis[...], nb[4], (((0,), (0,)), ((), ())), preferred_element_type=F32
    ).astype(BF16)

    def far_wide(d):
        return remote(
            win.at[centre], win.at[centre - d], ws.at[REACH - d], wr.at[REACH - d], w + d, c
        )

    for d in (1, -1, 2, -2, 3, -3):
        pl.when(within[d])(far_wide(d).start)
    for d in (-1, 1):
        pl.when(within[d])(near_to(d, 0, 4).start)

    def on_grid(a):
        return (w + a - REACH >= 0) & (w + a - REACH < wide)

    def hand_on(direction, k, j):
        held = REACH - direction * (k - 1)
        lands = held - direction
        a = REACH * core + j
        return remote(
            win.at[held * SPAN + a], win.at[lands * SPAN + a],
            rs.at[lands * (REACH + 1) + j], rr.at[lands * (REACH + 1) + j], w, c + direction,
        )

    def jump(direction, j):
        lands = REACH - direction * REACH
        a = REACH * core + j
        return remote(
            win.at[(REACH + direction) * SPAN + a], win.at[lands * SPAN + a],
            rs.at[lands * (REACH + 1) + j], rr.at[lands * (REACH + 1) + j],
            w, c + direction * (REACH + 1),
        )

    def jumps(direction):
        return c + REACH + 1 < col if direction > 0 else c - REACH - 1 >= 0

    def from_end(direction, j):
        lands = REACH - direction * REACH
        a = REACH * core + j
        return remote(
            win.at[REACH * SPAN + a], win.at[lands * SPAN + a],
            es.at[lands * (REACH + 1) + j], rr.at[lands * (REACH + 1) + j],
            w, c + direction * REACH,
        )

    def at_end(direction):
        if direction > 0:
            return (c == 0) & (c + REACH < col)
        return (c == col - 1) & (c - REACH >= 0)

    def share(i, j):
        return remote(
            win.at[i * SPAN + 1 + 2 * core + j], win.at[i * SPAN + (REACH + 1) * core + j],
            ps.at[i * REACH + j], pr.at[i * REACH + j], partner, c,
        )

    def arrives(direction, k):
        return c - k >= 0 if direction > 0 else c + k < col

    def sends(direction, k):
        held = c - (k - 1) >= 0 if direction > 0 else c + (k - 1) < col
        return held & beside[direction]

    def each(count, body):
        def run(j, carry):
            body(j)
            return carry

        lax.fori_loop(0, count, run, 0)

    def pass_on(direction, k):
        def row(j):
            here = arrives(direction, k) & on_grid(REACH * core + j)

            @pl.when(here)
            def _():
                hand_on(direction, k, j).wait_recv()

            if k == 1:
                @pl.when(here & jumps(-direction))
                def _():
                    jump(-direction, j).start()

            if k + 1 < REACH:
                @pl.when(sends(direction, k + 1) & on_grid(REACH * core + j))
                def _():
                    hand_on(direction, k + 1, j).start()

        each(REACH + 1, row)
        i = REACH - direction * k

        def across(j):
            @pl.when(arrives(direction, k) & on_grid(1 + 2 * core + j))
            def _():
                share(i, j).start()

        each(REACH, across)

    def take_share(direction, k):
        i = REACH - direction * k

        def row(j):
            @pl.when(arrives(direction, k) & on_grid((REACH + 1) * (1 - core) + j))
            def _():
                share(i, j).wait_recv()

        each(REACH, row)

    def far_strip(i):
        total = None
        for a in range(SPAN):
            if abs(i - REACH) > 1 or abs(a - REACH) > 1:
                term = dot(coup[order[0, i * SPAN + a]], win[i * SPAN + a])
                total = term if total is None else total + term
        far[...] += total

    for d in within:
        pl.when(within[-d])(far_wide(d).wait_recv)

    def first_hand(j):
        for d in (1, -1):
            @pl.when(beside[d] & on_grid(REACH * core + j))
            def _(d=d):
                hand_on(d, 1, j).start()

            @pl.when(at_end(d) & on_grid(REACH * core + j))
            def _(d=d):
                from_end(d, j).start()

    each(REACH + 1, first_hand)

    loads[2].wait()
    wv[...] = dot(selfb[...], nb[4])

    for d in (-1, 1):
        pl.when(beside[d])(near_col(-d).wait_recv)
        for e in (-1, 1):
            pl.when(beside[d] & within[e])(near_to(e, d, 4 + d).start)

    loads[4].wait()
    coup[coup.shape[0] - 1] = jnp.zeros(coup.shape[1:], BF16)
    far[...] = jnp.zeros_like(far)
    far_strip(REACH)
    for d in (1, -1):
        pass_on(d, 1)
    for d in (1, -1):
        take_share(d, 1)
    far_strip(REACH - 1)
    far_strip(REACH + 1)
    for e in (-1, 1):
        for d in (-1, 0, 1):
            ok = within[-e] if d == 0 else within[-e] & beside[d]
            pl.when(ok)(near_to(e, d, 4 + d).wait_recv)
    loads[3].wait()

    at = []
    for slot in range(near_ids.shape[1]):
        cluster = near_ids[0, slot]
        place = (lax.div(cluster, col) - w + 1) * 3 + (lax.rem(cluster, col) - c + 1)
        at.append(jnp.where(cluster >= 0, jnp.minimum(jnp.maximum(place, 0), 8), 9))
    for k in range(rows // step):
        piece = slice(k * step, (k + 1) * step)
        total = None
        for slot, place in enumerate(at):
            term = dot(near[slot, piece, :], nb[place])
            total = term if total is None else total + term
        wv[piece, :] += total

    for d in (1, -1):
        pass_on(d, 2)
        pass_on(d, 3)
    for d in (1, -1):
        take_share(d, 2)
    far_strip(REACH - 2)
    far_strip(REACH + 2)
    for d in (1, -1):
        take_share(d, 3)
    far_strip(REACH - 3)
    far_strip(REACH + 3)
    wv[...] += dot(basis[...], far[...].astype(BF16))
    if first:
        pick_rows(starts, wv, stage)
    local_grams([v, wv] if first else [vprev, x, wv], wv, g)

    pl.when(has_prev)(out_prev.wait_send)
    pl.when(has_next)(out_next.wait_send)
    for d in (-1, 1):
        pl.when(beside[d])(near_col(d).wait_send)
        pl.when(within[d])(near_to(d, 0, 4).wait_send)
        for e in (-1, 1):
            pl.when(beside[d] & within[e])(near_to(e, d, 4 + d).wait_send)
    for d in within:
        pl.when(within[d])(far_wide(d).wait_send)
    for k in range(1, REACH + 1):
        for d in (1, -1):

            def sent(j, d=d, k=k):
                if k < REACH:
                    @pl.when(sends(d, k) & on_grid(REACH * core + j))
                    def _():
                        hand_on(d, k, j).wait_send()
                else:
                    @pl.when(arrives(-d, 1) & jumps(d) & on_grid(REACH * core + j))
                    def _():
                        jump(d, j).wait_send()

                    @pl.when(at_end(d) & on_grid(REACH * core + j))
                    def _():
                        from_end(d, j).wait_send()

            def shared(j, d=d, k=k):
                @pl.when(arrives(d, k) & on_grid(1 + 2 * core + j))
                def _():
                    share(REACH - d * k, j).wait_send()

            each(REACH + 1, sent)
            each(REACH, shared)

    copies = halo_copies(stage, halo_w, hs, hr, w, c, col) if first else ()
    all_reduce(w, c, wide, col, g, half, land, ysl, gram, send, recv, copies)


def inverse_factors(matrices, scratch):
    n = matrices[0].shape[0]
    row = lax.broadcasted_iota(jnp.int32, (n, n), 0)
    lane = lax.broadcasted_iota(jnp.int32, (n, n), 1)
    eye = (row == lane).astype(F32)

    def lower(e):
        return jnp.where(row > lane, e, 0.5 * e * eye)

    scaled, scales = [], []
    for i, a in enumerate(matrices):
        only = a * eye
        by_row = lax.rsqrt(jnp.sum(only, axis=1, keepdims=True))
        by_lane = lax.rsqrt(jnp.sum(only, axis=0, keepdims=True))
        a = a * by_row * by_lane
        scratch[i] = eye - lower(a - eye)
        scaled.append(a)
        scales.append(by_lane)
    limit = 1e-5

    def go_on(state):
        step, error = state
        return (step < 8) & jnp.logical_not(error < limit)

    def refine(state):
        step, _ = state
        error = jnp.float32(0.0)
        for i, a in enumerate(scaled):
            m = scratch[i]
            e = dot_full_t(dot_full(m, a), m) - eye
            scratch[i] = m - dot_three(lower(e), m)
            error = error + jnp.sum(e * e)
        return step + 1, error

    _, error = lax.while_loop(go_on, refine, (jnp.int32(0), jnp.float32(1.0)))

    @pl.when(jnp.logical_not(error < limit))
    def _():
        for i, a in enumerate(scaled):

            def eliminate(j, state):
                s, m = state
                at_lane = jnp.sum(jnp.where(lane == j, s, 0.0), axis=1, keepdims=True)
                at_row = jnp.sum(jnp.where(row == j, s, 0.0), axis=0, keepdims=True)
                m_row = jnp.sum(jnp.where(row == j, m, 0.0), axis=0, keepdims=True)
                pivot = jnp.sum(jnp.where(row == j, at_lane, 0.0), axis=0, keepdims=True)
                pivot = pivot[:, 0:1]
                times = jnp.where(row[:, 0:1] > j, at_lane / pivot, 0.0)
                s = s - times * at_row
                m = m - times * m_row
                m = jnp.where(row == j, m_row * lax.rsqrt(pivot), m)
                return s, m

            _, m = lax.fori_loop(0, n, eliminate, (a, eye))
            scratch[i] = m

    for i, by_lane in enumerate(scales):
        scratch[i] = scratch[i] * by_lane


def first_factor_kernel(col, far_ids, g0, m, mt, order):
    w, c = lax.axis_index("wide"), lax.axis_index("col")
    slots = far_ids.shape[1]

    def clear(p, carry):
        order[0, p] = slots
        return carry

    def put(s, carry):
        cluster = far_ids[0, s]

        @pl.when(cluster >= 0)
        def _():
            dc = lax.rem(cluster, col) - c + REACH
            dw = lax.div(cluster, col) - w + REACH
            order[0, dc * SPAN + dw] = s

        return carry

    lax.fori_loop(0, SPAN * SPAN, clear, 0)
    lax.fori_loop(0, slots, put, 0)
    inverse_factors([g0[...]], m)
    mt[...] = m[0].T


def second_factor_kernel(gram, m, mt, u):
    k = gram.shape[1]
    h = gram[0:k, :]
    n = gram[k:, :]
    inverse_factors([n - t_dot_full(h, h), n], m)
    mt[...] = m[0].T
    u[...] = -dot_full(h, mt[...])


def last_kernel(step, g0, m0, gram1, mn, gram2, z1, z2, out, m):
    k = g0.shape[1]
    down = ((0,), (0,))
    beta = dot_three(m0[0], g0[...])
    h1, h2 = gram1[0:k, :], gram2[0:k, :]
    n12, n22 = gram2[k : 2 * k, :], gram2[2 * k :, :]
    first = mn[1]
    b1 = dot_three(first, dot_three(h1, beta, down))
    t = dot_full(first, n12)
    inverse_factors([n22 - t_dot_full(t, t)], m)
    b2 = dot_three(h2, beta, down) - dot_three(t, b1, down)
    y2 = dot_three(m[0], dot_three(m[0], b2), down)
    y1 = dot_three(first, b1 - dot_three(t, y2), down)

    def combine(i, carry):
        piece = pl.ds(pl.multiple_of(i * step, step), step)
        out[piece, :] = dot_three(z1[piece, :], y1) + dot_three(z2[piece, :], y2)
        return carry

    lax.fori_loop(0, out.shape[0] // step, combine, 0)


def on_device(
    wide, col, rhs, basis, self_block, near_block, near_ids, couplings, far_ids, starts, schwarz_inverse
):
    rows, width = rhs.shape
    rank = basis.shape[1]
    order = schwarz_inverse.shape[1]
    margin = (order - rows) // 2
    step = rows // 3
    slots, links = near_ids.shape[1], far_ids.shape[1]
    vmem = pl.BlockSpec(memory_space=pltpu.VMEM)
    smem = pl.BlockSpec(memory_space=pltpu.SMEM)
    anywhere = pl.BlockSpec(memory_space=pl.ANY)

    def block(n):
        return jax.ShapeDtypeStruct((n, width), F32)

    square = jax.ShapeDtypeStruct((1, width, width), F32)
    local = pltpu.CompilerParams(vmem_limit_bytes=VMEM_BYTES)

    def talks(number):
        return pltpu.CompilerParams(
            collective_id=number, has_side_effects=True, vmem_limit_bytes=VMEM_BYTES
        )

    halo = jax.ShapeDtypeStruct((2, margin, width), F32)
    gram0, halo_x = pl.pallas_call(
        functools.partial(first_gram_kernel, wide, col, step),
        out_shape=(block(width), halo),
        in_specs=[smem, vmem],
        out_specs=(vmem, vmem),
        scratch_shapes=[
            pltpu.VMEM((2, margin, width), F32),
            pltpu.SemaphoreType.DMA((2,)),
            pltpu.SemaphoreType.DMA((2,)),
        ]
        + reduce_scratch(width, width, wide, col),
        compiler_params=talks(0),
        name="first_gram",
    )(starts, rhs)
    m0, mt0, listed = pl.pallas_call(
        functools.partial(first_factor_kernel, col),
        out_shape=(square, block(width), jax.ShapeDtypeStruct((1, SPAN * SPAN), jnp.int32)),
        in_specs=[smem, vmem],
        out_specs=(vmem, vmem, smem),
        compiler_params=local,
        name="first_factor",
    )(far_ids, gram0)

    def take_step(first, *blocks):
        grams = 2 if first else 3
        outs = [block(rows)] * 3 + [halo] * 2 if first else [block(rows)]
        held = [] if first else [pltpu.VMEM((rows, width), F32)] * 2
        dma = pltpu.SemaphoreType.DMA
        return pl.pallas_call(
            functools.partial(step_kernel, wide, col, step, first),
            out_shape=(*outs, block(grams * width)),
            in_specs=[smem] * 3 + [vmem] * len(blocks) + [anywhere] * 5,
            out_specs=(vmem,) * (len(outs) + 1),
            scratch_shapes=held
            + [
                pltpu.VMEM((rows, rank), BF16),
                pltpu.VMEM((rows, rows), BF16),
                pltpu.VMEM((slots, rows, rows), BF16),
                pltpu.VMEM((links + 1, rank, rank), BF16),
                pltpu.VMEM((order, order), BF16),
                pltpu.VMEM((2, margin, width), F32),
                pltpu.VMEM((order, width), BF16),
                pltpu.VMEM((margin, width), F32),
                pltpu.VMEM((margin, width), F32),
                pltpu.VMEM((2, margin, width), F32),
                pltpu.VMEM((10, rows, width), BF16),
                pltpu.VMEM((SPAN * SPAN, rank, width), BF16),
                pltpu.VMEM((rank, width), F32),
                dma((5,)),
                dma((4,)),
                dma((4,)),
                dma((9,)),
                dma((9,)),
                dma((SPAN,)),
                dma((SPAN,)),
                dma((SPAN * (REACH + 1),)),
                dma((SPAN * (REACH + 1),)),
                dma((SPAN * (REACH + 1),)),
                dma((SPAN * REACH,)),
                dma((SPAN * REACH,)),
            ]
            + reduce_scratch(grams * width, width, wide, col),
            compiler_params=talks(1 if first else 2),
            name="first_step" if first else "second_step",
        )(starts, near_ids, listed, *blocks, basis, self_block, near_block, couplings, schwarz_inverse)

    v1, z1, w1, halo_v, halo_w, gram1 = take_step(True, rhs, mt0, halo_x)
    m1, mt1, u = pl.pallas_call(
        second_factor_kernel,
        out_shape=(jax.ShapeDtypeStruct((2, width, width), F32), block(width), block(width)),
        in_specs=[vmem],
        out_specs=(vmem,) * 3,
        compiler_params=local,
        name="second_factor",
    )(gram1)
    z2, gram2 = take_step(False, w1, mt1, halo_w, v1, u, halo_v)
    return pl.pallas_call(
        functools.partial(last_kernel, step),
        out_shape=block(rows),
        in_specs=[vmem] * 7,
        out_specs=vmem,
        scratch_shapes=[pltpu.VMEM((1, width, width), F32)],
        compiler_params=local,
        name="last",
    )(gram0, m0, gram1, m1, gram2, z1, z2)


def solution(mesh):
    in_specs = (
        P(("wide", "col"), None),
        P(("wide", "col"), None),
        P(("wide", "col"), None),
        P(("wide", "col"), None, None, None),
        P(("wide", "col"), None),
        P(("wide", "col"), None, None, None),
        P(("wide", "col"), None),
        P(("wide", "col"), None),
        P(("wide", "col"), None, None),
    )
    out_specs = P(("wide", "col"), None)
    return jax.shard_map(
        functools.partial(on_device, mesh.shape["wide"], mesh.shape["col"]),
        mesh=mesh,
        in_specs=in_specs,
        out_specs=out_specs,
        check_vma=False,
    )
```
